256 devices in a mesh: pts: 16 (over z, core), hrs: 8 (over y_hi, x), bins: 2 (over y_lo).
Axes of the slice: x: 4, y: 4 (y_hi: 2, y_lo: 2; y = y_hi * 2 + y_lo), z: 8, core: 2. Of those that a mesh axis runs over, the one named last changes fastest.
Arguments:
- tensor: float32 [128, 4096, 1296], P('hrs', 'pts', 'bins'), may hold values from -6 to 6
- b_factor: float32 [4096, 256], P(('pts', 'hrs')), as said below
- c_factor: float32 [1296, 256], P('bins'), as said below
Outputs:
- hour_factor: float32 [128, 256], P('hrs')
- point_factor: float32 [4096, 256], P(('pts', 'hrs'))
The draws below stay inside these ranges and needn't reach their ends.
Inputs may be any that keep to these rules, and one draw needn't show every extreme that they name: `b_factor`: real-valued factor rows. `c_factor`: real-valued factor rows.
All inputs are finite; a program needn't handle non-finite values.
Results may differ from the reference program's by a relative error of at most 0.00018.
Values sent between devices are 32-bit elements; how exact they have to be, the bound alone decides.
A program may use at most 64 MiB of HBM per device.

```python
import math
import jax
import jax.numpy as jnp
from jax import lax

K = 1296
RANK = 256
I = 128
J = 4096


def shape_rows(jitter, key_common, key_spread, common_share, count):
    common = jax.random.normal(key_common, (count, 1), jnp.float32)
    ramp_rows = 1.0 + 2.0 * jnp.arange(count, dtype=jnp.float32)[:, None] / count
    spread = jnp.exp(jax.random.uniform(key_spread, (count, 1), jnp.float32, 0.0, math.log(10.0)))
    return spread * ramp_rows * (jitter + common_share * common) / (9.5 * math.sqrt(count))


def draw_b_factor(key, part):
    key = jax.random.fold_in(key, 11)
    key_jitter, key_common, key_spread = jax.random.split(key, 3)
    jitter = jax.random.normal(key_jitter, (J, RANK), jnp.float32)
    share = 0.6
    return shape_rows(jitter, key_common, key_spread, share, J)


def draw_c_factor(key, part):
    key = jax.random.fold_in(key, 23)
    key_jitter, key_common, key_spread = jax.random.split(key, 3)
    jitter = jax.random.normal(key_jitter, (K, RANK), jnp.float32)
    share = 0.6
    return shape_rows(jitter, key_common, key_spread, share, K)


def level_of(stream_key, extent, cuts, low, top_value):
    factor_of = 1.0
    for position, shards_of in cuts:
        heights = jax.random.uniform(jax.random.fold_in(jax.random.fold_in(stream_key, 6), position), (shards_of,), jnp.float32, low / len(cuts), top_value / len(cuts))
        factor_of = factor_of * jnp.repeat(jnp.exp(heights), extent[position] // shards_of).reshape((-1,) + (1,) * (len(extent) - 1 - position))
    return factor_of


def normal_values(key, shape, deviation, limit, cuts=(), kind=jnp.bfloat16):
    values = deviation * jax.random.normal(key, shape, jnp.float32)
    if cuts:
        values = values * level_of(key, shape, cuts, -0.22, 0.18)
    return jnp.clip(values, -limit, limit).astype(kind)


def setup_inputs(seed: int = 0) -> dict:
    arg_keys = jax.random.split(jax.random.key(seed), 4)
    return {
        "tensor": normal_values(arg_keys[0], (I, J, K), 1.0, 6.0, ((0, 8), (1, 16), (2, 2)), jnp.float32),
        "b_factor": draw_b_factor(jax.random.fold_in(arg_keys[3], 71), 0),
        "c_factor": draw_c_factor(jax.random.fold_in(arg_keys[3], 71), 0),
    }


def normal_solve(rhs, hadamard):
    factor = jnp.linalg.cholesky(hadamard)
    return jax.scipy.linalg.cho_solve((factor, True), rhs.T).T

def reference(tensor, b_factor, c_factor):
    highest = lax.Precision.HIGHEST
    gram_c = jnp.dot(c_factor.T, c_factor, precision=highest)
    gram_b = jnp.dot(b_factor.T, b_factor, precision=highest)
    contracted = jnp.dot(tensor.reshape(I * J, K), c_factor, precision=highest).reshape(I, J, RANK)
    mttkrp_hours = jnp.einsum('ijr,jr->ir', contracted, b_factor, precision=highest)
    hour_factor = normal_solve(mttkrp_hours, gram_b * gram_c)
    gram_a = jnp.dot(hour_factor.T, hour_factor, precision=highest)
    mttkrp_points = jnp.einsum('ijr,ir->jr', contracted, hour_factor, precision=highest)
    point_factor = normal_solve(mttkrp_points, gram_a * gram_c)
    return (hour_factor, point_factor)
```

```python
import functools

import jax
import jax.numpy as jnp
from jax import lax
from jax.experimental import pallas as pl
from jax.experimental.pallas import tpu as pltpu
from jax.sharding import PartitionSpec as P

f32 = jnp.float32
bf16 = jnp.bfloat16
HIGHEST = lax.Precision.HIGHEST
MESH = pl.DeviceIdType.MESH
CONTRACT_ROWS = (((0,), (0,)), ((), ()))


def gram(x):
    return lax.dot_general(
        x, x, CONTRACT_ROWS, precision=HIGHEST, preferred_element_type=f32
    )


def split(x):
    first = x.astype(bf16).astype(f32)
    rest = x - first
    second = rest.astype(bf16).astype(f32)
    return first, second, rest - second


def reciprocal(x):
    y = pltpu.reciprocal(x, approx=True)
    y = y * (2.0 - x * y)
    return y * (2.0 - x * y)


def eliminate(k, a):
    width = a.shape[1]
    row = pl.multiple_of(k * 8, 8)
    panel = a[pl.ds(row, 8), :]
    tile = pl.multiple_of((k // 16) * 128, 128)
    pivots = pltpu.roll(
        a[pl.ds(row, 8), pl.ds(tile, 128)], lax.rem(128 - lax.rem(k, 16) * 8, 128), 1
    )
    lane = lax.broadcasted_iota(jnp.int32, (8, width), 1)
    sub = lax.broadcasted_iota(jnp.int32, (8, width), 0)
    sub1 = lax.broadcasted_iota(jnp.int32, (8, 128), 0)
    rel = lane - row
    inside = (rel >= 0) & (rel < 8)
    column = jnp.where(lane < row, -panel, panel)
    work = jnp.where(inside, jnp.where(rel == sub, 1.0, 0.0), panel)
    cols = [jnp.broadcast_to(pivots[:, j : j + 1], (8, 128)) for j in range(8)]
    data = [work[:, s : s + 128] for s in range(0, width, 128)]
    for j in range(8):
        state = cols[j:] + data
        rows = [jnp.broadcast_to(x[j : j + 1, :], (8, 128)) for x in state]
        inverse = reciprocal(rows[0])
        factor = jnp.where(sub1 == j, 1.0 - inverse, cols[j] * inverse)
        state = [x - factor * r for x, r in zip(state, rows)]
        cols = cols[:j] + state[: 8 - j]
        data = state[8 - j :]
    panel = jnp.concatenate(data, axis=1)
    c1, c2, c3 = split(column)
    r1, r2, r3 = split(panel)
    left = jnp.concatenate([c1, c1, c2, c2, c1, c3], axis=0).astype(bf16)
    right = jnp.concatenate([r1, r2, r1, r2, r3, r1], axis=0).astype(bf16)
    update = lax.dot_general(
        left, right, CONTRACT_ROWS, preferred_element_type=f32
    )
    rel = lax.broadcasted_iota(jnp.int32, a.shape, 1) - row
    a[...] = jnp.where((rel >= 0) & (rel < 8), 0.0, a[...]) - update
    a[pl.ds(row, 8), :] = panel


def kernel(
    sizes,
    t_hbm,
    b_hbm,
    c_hbm,
    hf_ref,
    pf_ref,
    tbuf,
    con,
    cbuf,
    chi,
    clo,
    bbuf,
    gb_part,
    gc_part,
    gb_in,
    gc_in,
    gb_z,
    hmat,
    gcm,
    mh,
    mh_core,
    mh_mine,
    mh_bins,
    mh_z,
    mh_all,
    hfall,
    mp,
    mp_in,
    owned,
    lsem,
    ssem,
    rsem,
):
    NP, NH, NB = sizes
    Z, Q = NP // 2, NH * NB
    hours, points, _ = t_hbm.shape
    width = c_hbm.shape[1]
    half = width // 2
    prow = half // Q
    brow = b_hbm.shape[0]
    mrow = points // Q
    hh = hours // 2
    p, h, n = lax.axis_index("pts"), lax.axis_index("hrs"), lax.axis_index("bins")
    z, core = p // 2, lax.rem(p, 2)
    q = h * NB + n

    def plane(d):
        t = lax.rem(q + d, Q)
        return (p, t // NB, lax.rem(t, NB))

    def along_hours(d):
        return (p, lax.rem(h + d, NH), n)

    def along_z(d):
        return (lax.rem(z + d, Z) * 2 + core, h, n)

    other_core = (p + 1 - 2 * core, h, n)
    other_bins = (p, h, 1 - n)

    def remote(src, dst, i, target):
        return pltpu.make_async_remote_copy(
            src_ref=src,
            dst_ref=dst,
            send_sem=ssem.at[i],
            recv_sem=rsem.at[i],
            device_id=target,
            device_id_type=MESH,
        )

    def start_all(count, make):
        def body(d, _):
            make(d).start()
            return 0

        lax.fori_loop(1, count, body, 0)

    def wait_all(count, make):
        def body(d, _):
            make(d).wait()
            return 0

        lax.fori_loop(1, count, body, 0)

    load_b = pltpu.make_async_copy(
        b_hbm, bbuf.at[pl.ds(pl.multiple_of(h * brow, 8), brow)], lsem.at[hours]
    )
    load_c = pltpu.make_async_copy(c_hbm, cbuf, lsem.at[hours + 1])
    load_b.start()
    load_c.start()

    def load_t(i):
        return pltpu.make_async_copy(t_hbm.at[i], tbuf.at[i], lsem.at[i])

    def start_t(i, _):
        load_t(i).start()
        return 0

    lax.fori_loop(0, hours, start_t, 0)

    barrier = pltpu.get_barrier_semaphore()

    def greet(make):
        def body(d, _):
            pl.semaphore_signal(
                barrier, inc=1, device_id=make(d), device_id_type=MESH
            )
            return 0

        return body

    lax.fori_loop(1, Q, greet(plane), 0)
    lax.fori_loop(1, Z, greet(along_z), 0)
    pl.semaphore_signal(barrier, inc=1, device_id=other_core, device_id_type=MESH)
    pl.semaphore_wait(barrier, Q + Z - 1)

    base = 0

    my_b = pl.ds(pl.multiple_of(h * brow, 8), brow)
    send_b = lambda d: remote(bbuf.at[my_b], bbuf.at[my_b], d, along_hours(d))
    base += NH
    load_b.wait()
    start_all(NH, send_b)

    load_c.wait()
    c = cbuf[...]
    gc_part[...] = gram(c)
    hi = c.astype(bf16)
    chi[...] = hi
    clo[...] = (c - hi.astype(f32)).astype(bf16)
    my_rows = pl.ds(pl.multiple_of(half * core + prow * q, 8), prow)
    q_bins = h * NB + 1 - n
    bins_rows = pl.ds(pl.multiple_of(half * core + prow * q_bins, 8), prow)
    send_gc = remote(gc_part.at[bins_rows], gc_in, base, other_bins)
    base += 1
    send_gc.start()

    def contract(i, _):
        load_t(i).wait()
        x = tbuf[i]
        xh = x.astype(bf16)
        xl = (x - xh.astype(f32)).astype(bf16)
        dot = functools.partial(jnp.dot, preferred_element_type=f32)
        con[i] = dot(xh, chi[...]) + (dot(xh, clo[...]) + dot(xl, chi[...]))
        return 0

    wait_all(NH, send_b)
    gb_part[...] = gram(bbuf[...])
    core_rows = pl.ds(pl.multiple_of(half * (1 - core) + prow * q, 8), prow)
    send_gb = remote(gb_part.at[core_rows], gb_in, base, other_core)
    base += 1
    send_gb.start()

    send_gc.wait()
    gcm[my_rows, :] = gc_part[my_rows, :] + gc_in[...]
    gc_base = base
    send_gcm = lambda d: remote(gcm.at[my_rows], gcm.at[my_rows], gc_base + d, plane(d))
    base += Q
    start_all(Q, send_gcm)

    send_gb.wait()
    gb_z[z] = gb_part[my_rows, :] + gb_in[...]
    z_base = base
    send_gbz = lambda d: remote(gb_z.at[z], gb_z.at[z], z_base + d, along_z(d))
    base += Z
    start_all(Z, send_gbz)

    lax.fori_loop(0, hours // 2, contract, 0)

    wait_all(Z, send_gbz)
    total = gb_z[0]
    for s in range(1, Z):
        total = total + gb_z[s]
    hmat[my_rows, :] = total * gcm[my_rows, :]
    h_base = base
    send_h = lambda d: remote(hmat.at[my_rows], hmat.at[my_rows], h_base + d, plane(d))
    base += Q
    start_all(Q, send_h)

    lax.fori_loop(hours // 2, hours, contract, 0)

    wait_all(Q, send_h)
    my_half = pl.ds(pl.multiple_of(half * core, 8), half)
    swap_h = remote(hmat.at[my_half], hmat.at[my_half], base, other_core)
    base += 1
    swap_h.start()
    wait_all(Q, send_gcm)
    swap_gc = remote(gcm.at[my_half], gcm.at[my_half], base, other_core)
    base += 1
    swap_gc.start()

    def partial_hours(i, _):
        mh[pl.ds(i, 1), :] = jnp.sum(con[i] * bbuf[...], axis=0, keepdims=True)
        return 0

    lax.fori_loop(0, hours, partial_hours, 0)
    keep = pl.ds(pl.multiple_of(hh * core, 8), hh)
    give = pl.ds(pl.multiple_of(hh * (1 - core), 8), hh)
    send_mc = remote(mh.at[give], mh_core, base, other_core)
    base += 1
    send_mc.start()

    blocks = width // 8
    marks = [0, blocks // 8, blocks // 4, blocks * 5 // 8, blocks]

    def run(s):
        def body(k, _):
            eliminate(k, hmat)
            return 0

        lax.fori_loop(marks[s], marks[s + 1], body, 0)

    swap_h.wait()
    run(0)
    send_mc.wait()
    mh_mine[...] = mh[keep, :] + mh_core[...]
    send_mb = remote(mh_mine, mh_bins, base, other_bins)
    base += 1
    send_mb.start()
    run(1)
    send_mb.wait()
    mh_z[z] = mh_mine[...] + mh_bins[...]
    mz_base = base
    send_mz = lambda d: remote(mh_z.at[z], mh_z.at[z], mz_base + d, along_z(d))
    base += Z
    start_all(Z, send_mz)
    run(2)
    wait_all(Z, send_mz)
    total = mh_z[0]
    for s in range(1, Z):
        total = total + mh_z[s]
    mh_all[keep, :] = total
    swap_m = remote(mh_all.at[keep], mh_all.at[keep], base, other_core)
    base += 1
    swap_m.start()
    run(3)
    swap_m.wait()

    hf = jnp.dot(
        mh_all[...], hmat[...], precision=HIGHEST, preferred_element_type=f32
    )
    my_hours = pl.ds(pl.multiple_of(h * hours, 8), hours)
    hfall[my_hours, :] = hf
    hf_base = base
    send_hf = lambda d: remote(
        hfall.at[my_hours], hfall.at[my_hours], hf_base + d, along_hours(d)
    )
    base += NH
    start_all(NH, send_hf)
    hf_ref[...] = hf

    def piece(t):
        rows = pl.ds(pl.multiple_of(t * mrow, 8), mrow)
        acc = con[0, rows, :] * hf[0:1, :]
        for i in range(1, hours):
            acc = acc + con[i, rows, :] * hf[i : i + 1, :]
        return acc

    mp_base = base
    send_mp = lambda d: remote(mp.at[d], mp_in.at[d], mp_base + d, plane(d))
    base += Q

    def points_body(d, _):
        mp[d] = piece(lax.rem(q + d, Q))
        send_mp(d).start()
        return 0

    lax.fori_loop(1, Q, points_body, 0)
    mp_in[0] = piece(q)

    wait_all(NH, send_hf)
    swap_gc.wait()
    hmat[...] = gram(hfall[...]) * gcm[...]
    run(0)
    run(1)
    wait_all(Q, send_mp)
    total = mp_in[0]
    for s in range(1, Q):
        total = total + mp_in[s]
    mine = pl.ds(pl.multiple_of(n * mrow, 8), mrow)
    owned[mine, :] = total
    swap_o = remote(owned.at[mine], owned.at[mine], base, other_bins)
    base += 1
    swap_o.start()
    run(2)
    run(3)
    swap_o.wait()
    pf_ref[...] = jnp.dot(
        owned[...], hmat[...], precision=HIGHEST, preferred_element_type=f32
    )


def local(sizes, tensor, b_factor, c_factor):
    NP, NH, NB = sizes
    Z, Q = NP // 2, NH * NB
    hours, points, bins = tensor.shape
    width = c_factor.shape[1]
    brow = b_factor.shape[0]
    prow = width // (2 * Q)
    mrow = points // Q
    hh = hours // 2
    sems = NH + 1 + 1 + Q + Z + Q + 2 + 1 + 1 + Z + 1 + NH + Q + 1
    vm = lambda *shape: pltpu.VMEM(shape, f32)
    any_spec = pl.BlockSpec(memory_space=pl.ANY)
    vmem_spec = pl.BlockSpec(memory_space=pltpu.VMEM)
    return pl.pallas_call(
        functools.partial(kernel, sizes),
        out_shape=(
            jax.ShapeDtypeStruct((hours, width), f32),
            jax.ShapeDtypeStruct((brow, width), f32),
        ),
        in_specs=[any_spec] * 3,
        out_specs=(vmem_spec, vmem_spec),
        scratch_shapes=[
            vm(hours, points, bins),
            vm(hours, points, width),
            vm(bins, width),
            pltpu.VMEM((bins, width), bf16),
            pltpu.VMEM((bins, width), bf16),
            vm(points, width),
            vm(width, width),
            vm(width, width),
            vm(prow, width),
            vm(prow, width),
            vm(Z, prow, width),
            vm(width, width),
            vm(width, width),
            vm(hours, width),
            vm(hh, width),
            vm(hh, width),
            vm(hh, width),
            vm(Z, hh, width),
            vm(hours, width),
            vm(hours * NH, width),
            vm(Q, mrow, width),
            vm(Q, mrow, width),
            vm(brow, width),
            pltpu.SemaphoreType.DMA((hours + 2,)),
            pltpu.SemaphoreType.DMA((sems,)),
            pltpu.SemaphoreType.DMA((sems,)),
        ],
        compiler_params=pltpu.CompilerParams(
            collective_id=0,
            has_side_effects=True,
            vmem_limit_bytes=40 * 1024 * 1024,
        ),
    )(tensor, b_factor, c_factor)


def solution(mesh):
    sizes = (mesh.shape["pts"], mesh.shape["hrs"], mesh.shape["bins"])
    placed = (P("hrs", "pts", "bins"), P(("pts", "hrs"), None), P("bins", None))
    return jax.shard_map(
        functools.partial(local, sizes),
        mesh=mesh,
        in_specs=placed,
        out_specs=(P("hrs", None), P(("pts", "hrs"), None)),
        check_vma=False,
    )
```

```python
import functools

import jax
import jax.numpy as jnp
from jax import lax
from jax.experimental import pallas as pl
from jax.experimental.pallas import tpu as pltpu
from jax.sharding import PartitionSpec as P

f32 = jnp.float32
bf16 = jnp.bfloat16
HIGHEST = lax.Precision.HIGHEST
MESH = pl.DeviceIdType.MESH
CONTRACT_ROWS = (((0,), (0,)), ((), ()))


def gram(x):
    return lax.dot_general(
        x, x, CONTRACT_ROWS, precision=HIGHEST, preferred_element_type=f32
    )


def split(x):
    first = x.astype(bf16).astype(f32)
    rest = x - first
    second = rest.astype(bf16).astype(f32)
    return first, second, rest - second


STEP = 16


def spread_lanes(x, first):
    return [
        jnp.take_along_axis(
            x,
            jnp.full(x.shape, first + j, jnp.int32),
            axis=1,
            mode="promise_in_bounds",
        )
        for j in range(STEP)
    ]


def spread_row(x, j):
    return jnp.broadcast_to(x[j : j + 1, :], x.shape)


def lane_tile(x, t):
    return jnp.where(t == 0, x[:, :128], x[:, 128:])


def pivot(panel, row):
    lane = lax.broadcasted_iota(jnp.int32, panel.shape, 1)
    sub = lax.broadcasted_iota(jnp.int32, panel.shape, 0)
    rel = lane - row
    t = row // 128
    cols = spread_lanes(lane_tile(panel, t), row - t * 128)
    work = jnp.where((rel >= 0) & (rel < STEP), jnp.where(rel == sub, 1.0, 0.0), panel)
    data = [work[:, :128], work[:, 128:]]
    sub = lax.broadcasted_iota(jnp.int32, (STEP, 128), 0)
    for j in range(STEP):
        state = cols[j:] + data
        rows = [spread_row(x, j) for x in state]
        inverse = pltpu.reciprocal(rows[0], approx=False)
        factor = jnp.where(sub == j, 1.0 - inverse, cols[j] * inverse)
        state = [x - factor * r for x, r in zip(state, rows)]
        cols = cols[:j] + state[: STEP - j]
        data = state[STEP - j :]
    column = jnp.where(lane < row, -panel, panel)
    return jnp.concatenate(data, axis=1), column


def follow(rows, done, row):
    rel = lax.broadcasted_iota(jnp.int32, rows.shape, 1) - row
    t = row // 128
    cols = spread_lanes(lane_tile(rows, t), row - t * 128)
    rows = jnp.where((rel >= 0) & (rel < STEP), 0.0, rows)
    out = []
    for s in (0, 128):
        part = done[:, s : s + 128]
        terms = [cols[j] * spread_row(part, j) for j in range(STEP)]
        while len(terms) > 1:
            terms = [x + y for x, y in zip(terms[::2], terms[1::2])]
        out.append(rows[:, s : s + 128] - terms[0])
    return jnp.concatenate(out, axis=1)


def factors(left, right, column, done):
    c1, c2, c3 = split(column)
    r1, r2, r3 = split(done)
    left[...] = jnp.concatenate([c1, c1, c2, c2, c1, c3], axis=0).astype(bf16)
    right[...] = jnp.concatenate([r1, r2, r1, r2, r3, r1], axis=0).astype(bf16)


def late_update(a, left, right, row, done):
    update = lax.dot_general(
        left[...], right[...], CONTRACT_ROWS, preferred_element_type=f32
    )
    rel = lax.broadcasted_iota(jnp.int32, a.shape, 1) - row
    a[...] = jnp.where((rel >= 0) & (rel < STEP), 0.0, a[...]) - update
    a[pl.ds(row, STEP), :] = done


def invert(a, left, right, pauses):
    steps = a.shape[0] // STEP

    def at(k):
        return pl.multiple_of(k * STEP, STEP)

    done, column = pivot(a[0:STEP, :], 0)
    factors(left, right, column, done)
    panel = follow(a[STEP : 2 * STEP, :], done, 0)

    def body(k, carry):
        panel, before = carry
        late_update(a, left, right, at(k - 1), before)
        done, column = pivot(panel, at(k))
        panel = follow(a[pl.ds(at(k + 1), STEP), :], done, at(k))
        factors(left, right, column, done)
        return panel, done

    carry = (panel, done)
    first = 1
    for stop in sorted(pauses):
        carry = lax.fori_loop(first, stop, body, carry)
        pauses[stop]()
        first = stop
    panel, before = lax.fori_loop(first, steps - 1, body, carry)
    late_update(a, left, right, at(steps - 2), before)
    done, column = pivot(panel, at(steps - 1))
    factors(left, right, column, done)
    late_update(a, left, right, at(steps - 1), done)


def kernel(
    sizes,
    t_hbm,
    b_hbm,
    c_hbm,
    hf_ref,
    pf_ref,
    tbuf,
    con,
    cbuf,
    ct,
    bbuf,
    bt,
    gb_part,
    gc_part,
    gb_in,
    gc_in,
    gb_z,
    hmat,
    gcm,
    mht,
    mh,
    mh_core,
    mh_mine,
    mh_bins,
    mh_z,
    mh_all,
    hft,
    hfall,
    mpt,
    mp,
    mp_in,
    owned,
    left,
    right,
    lsem,
    ssem,
    rsem,
):
    NP, NH, NB = sizes
    Z, Q = NP // 2, NH * NB
    hours, _, points = t_hbm.shape
    width = c_hbm.shape[1]
    half = width // 2
    prow = half // Q
    brow = b_hbm.shape[0]
    mrow = points // Q
    hh = hours // 2
    p, h, n = lax.axis_index("pts"), lax.axis_index("hrs"), lax.axis_index("bins")
    z, core = p // 2, lax.rem(p, 2)
    q = h * NB + n

    def plane(d):
        t = lax.rem(q + d, Q)
        return (p, t // NB, lax.rem(t, NB))

    def along_hours(d):
        return (p, lax.rem(h + d, NH), n)

    def along_z(d):
        return (lax.rem(z + d, Z) * 2 + core, h, n)

    other_core = (p + 1 - 2 * core, h, n)
    other_bins = (p, h, 1 - n)

    def remote(src, dst, i, target):
        return pltpu.make_async_remote_copy(
            src_ref=src,
            dst_ref=dst,
            send_sem=ssem.at[i],
            recv_sem=rsem.at[i],
            device_id=target,
            device_id_type=MESH,
        )

    def start_all(count, make):
        def body(d, _):
            make(d).start()
            return 0

        lax.fori_loop(1, count, body, 0)

    def wait_all(count, make):
        def body(d, _):
            make(d).wait()
            return 0

        lax.fori_loop(1, count, body, 0)

    load_b = pltpu.make_async_copy(
        b_hbm, bbuf.at[pl.ds(pl.multiple_of(h * brow, 8), brow)], lsem.at[hours]
    )
    load_c = pltpu.make_async_copy(c_hbm, cbuf, lsem.at[hours + 1])
    load_b.start()
    load_c.start()

    def load_t(i):
        return pltpu.make_async_copy(t_hbm.at[i], tbuf.at[i], lsem.at[i])

    def start_t(i, _):
        load_t(i).start()
        return 0

    lax.fori_loop(0, hours, start_t, 0)

    barrier = pltpu.get_barrier_semaphore()

    def greet(make):
        def body(d, _):
            pl.semaphore_signal(
                barrier, inc=1, device_id=make(d), device_id_type=MESH
            )
            return 0

        return body

    lax.fori_loop(1, Q, greet(plane), 0)
    lax.fori_loop(1, Z, greet(along_z), 0)
    pl.semaphore_signal(barrier, inc=1, device_id=other_core, device_id_type=MESH)
    pl.semaphore_wait(barrier, Q + Z - 1)

    base = 0

    my_b = pl.ds(pl.multiple_of(h * brow, 8), brow)
    send_b = lambda d: remote(bbuf.at[my_b], bbuf.at[my_b], d, along_hours(d))
    base += NH
    load_b.wait()
    start_all(NH, send_b)

    load_c.wait()
    gc_part[...] = gram(cbuf[...])
    my_rows = pl.ds(pl.multiple_of(half * core + prow * q, 8), prow)
    q_bins = h * NB + 1 - n
    bins_rows = pl.ds(pl.multiple_of(half * core + prow * q_bins, 8), prow)
    send_gc = remote(gc_part.at[bins_rows], gc_in, base, other_bins)
    base += 1
    send_gc.start()
    c = cbuf[...].T
    hi = c.astype(bf16)
    ct[:width, :] = hi
    ct[width:, :] = (c - hi.astype(f32)).astype(bf16)

    def contract(i, _):
        load_t(i).wait()
        x = tbuf[i]
        xh = x.astype(bf16)
        xl = (x - xh.astype(f32)).astype(bf16)
        dot = functools.partial(jnp.dot, preferred_element_type=f32)
        chi, clo = ct[:width, :], ct[width:, :]
        con[i] = dot(chi, xh) + (dot(clo, xh) + dot(chi, xl))
        return 0

    wait_all(NH, send_b)
    gb_part[...] = gram(bbuf[...])
    bt[...] = bbuf[...].T
    core_rows = pl.ds(pl.multiple_of(half * (1 - core) + prow * q, 8), prow)
    send_gb = remote(gb_part.at[core_rows], gb_in, base, other_core)
    base += 1
    send_gb.start()

    send_gc.wait()
    gcm[my_rows, :] = gc_part[my_rows, :] + gc_in[...]
    gc_base = base
    send_gcm = lambda d: remote(gcm.at[my_rows], gcm.at[my_rows], gc_base + d, plane(d))
    base += Q
    start_all(Q, send_gcm)

    send_gb.wait()
    gb_z[z] = gb_part[my_rows, :] + gb_in[...]
    z_base = base
    send_gbz = lambda d: remote(gb_z.at[z], gb_z.at[z], z_base + d, along_z(d))
    base += Z
    start_all(Z, send_gbz)

    lax.fori_loop(0, hours // 2, contract, 0)

    wait_all(Z, send_gbz)
    total = gb_z[0]
    for s in range(1, Z):
        total = total + gb_z[s]
    hmat[my_rows, :] = total * gcm[my_rows, :]
    h_base = base
    send_h = lambda d: remote(hmat.at[my_rows], hmat.at[my_rows], h_base + d, plane(d))
    base += Q
    start_all(Q, send_h)

    lax.fori_loop(hours // 2, hours, contract, 0)

    wait_all(Q, send_h)
    my_half = pl.ds(pl.multiple_of(half * core, 8), half)
    swap_h = remote(hmat.at[my_half], hmat.at[my_half], base, other_core)
    base += 1
    swap_h.start()
    wait_all(Q, send_gcm)
    swap_gc = remote(gcm.at[my_half], gcm.at[my_half], base, other_core)
    base += 1
    swap_gc.start()

    lane = lax.broadcasted_iota(jnp.int32, mht.shape, 1)

    def partial_hours(i, _):
        prod = con[i] * bt[...]
        total = jnp.sum(prod, axis=1, keepdims=True)
        mht[...] = jnp.where(lane == i, total, mht[...])
        return 0

    lax.fori_loop(0, hours, partial_hours, 0)
    mh[...] = mht[...].T[:hours, :]
    keep = pl.ds(pl.multiple_of(hh * core, 8), hh)
    give = pl.ds(pl.multiple_of(hh * (1 - core), 8), hh)
    send_mc = remote(mh.at[give], mh_core, base, other_core)
    base += 1
    send_mc.start()

    send_mb = remote(mh_mine, mh_bins, base, other_bins)
    base += 1
    mz_base = base
    send_mz = lambda d: remote(mh_z.at[z], mh_z.at[z], mz_base + d, along_z(d))
    base += Z
    swap_m = remote(mh_all.at[keep], mh_all.at[keep], base, other_core)
    base += 1

    def pause_core():
        send_mc.wait()
        mh_mine[...] = mh[keep, :] + mh_core[...]
        send_mb.start()

    def pause_bins():
        send_mb.wait()
        mh_z[z] = mh_mine[...] + mh_bins[...]
        start_all(Z, send_mz)

    def pause_z():
        wait_all(Z, send_mz)
        total = mh_z[0]
        for s in range(1, Z):
            total = total + mh_z[s]
        mh_all[keep, :] = total
        swap_m.start()

    swap_h.wait()
    invert(hmat, left, right, {3: pause_core, 6: pause_bins, 11: pause_z})
    swap_m.wait()

    hf = jnp.dot(
        mh_all[...], hmat[...], precision=HIGHEST, preferred_element_type=f32
    )
    my_hours = pl.ds(pl.multiple_of(h * hours, 8), hours)
    hfall[my_hours, :] = hf
    hft[...] = hf.T
    hf_base = base
    send_hf = lambda d: remote(
        hfall.at[my_hours], hfall.at[my_hours], hf_base + d, along_hours(d)
    )
    base += NH
    start_all(NH, send_hf)
    hf_ref[...] = hf

    chunk = 32
    for rows in range(0, width, chunk):
        weights = hft[rows : rows + chunk, :]
        acc = con[0, rows : rows + chunk, :] * weights[:, 0:1]
        for i in range(1, hours):
            acc = acc + con[i, rows : rows + chunk, :] * weights[:, i : i + 1]
        mpt[rows : rows + chunk, :] = acc
    mp[...] = mpt[...].T
    mp_base = base

    def send_mp(d):
        t = lax.rem(q + d, Q)
        rows = pl.ds(pl.multiple_of(t * mrow, 8), mrow)
        return remote(mp.at[rows], mp_in.at[d], mp_base + d, plane(d))

    base += Q
    start_all(Q, send_mp)

    wait_all(NH, send_hf)
    swap_gc.wait()
    hmat[...] = gram(hfall[...]) * gcm[...]
    mine = pl.ds(pl.multiple_of(n * mrow, 8), mrow)
    swap_o = remote(owned.at[mine], owned.at[mine], base, other_bins)
    base += 1

    def pause_points():
        wait_all(Q, send_mp)
        total = mp[pl.ds(pl.multiple_of(q * mrow, 8), mrow), :]
        for s in range(1, Q):
            total = total + mp_in[s]
        owned[mine, :] = total
        swap_o.start()

    invert(hmat, left, right, {8: pause_points})
    swap_o.wait()
    pf_ref[...] = jnp.dot(
        owned[...], hmat[...], precision=HIGHEST, preferred_element_type=f32
    )


def local(sizes, tensor, b_factor, c_factor):
    NP, NH, NB = sizes
    Z, Q = NP // 2, NH * NB
    tensor = jnp.swapaxes(tensor, 1, 2)
    hours, bins, points = tensor.shape
    width = c_factor.shape[1]
    brow = b_factor.shape[0]
    prow = width // (2 * Q)
    mrow = points // Q
    hh = hours // 2
    sems = NH + 1 + 1 + Q + Z + Q + 2 + 1 + 1 + Z + 1 + NH + Q + 1
    vm = lambda *shape: pltpu.VMEM(shape, f32)
    any_spec = pl.BlockSpec(memory_space=pltpu.HBM)
    vmem_spec = pl.BlockSpec(memory_space=pltpu.VMEM)
    return pl.pallas_call(
        functools.partial(kernel, sizes),
        out_shape=(
            jax.ShapeDtypeStruct((hours, width), f32),
            jax.ShapeDtypeStruct((brow, width), f32),
        ),
        in_specs=[any_spec] * 3,
        out_specs=(vmem_spec, vmem_spec),
        scratch_shapes=[
            vm(hours, bins, points),
            vm(hours, width, points),
            vm(bins, width),
            pltpu.VMEM((2 * width, bins), bf16),
            vm(points, width),
            vm(width, points),
            vm(width, width),
            vm(width, width),
            vm(prow, width),
            vm(prow, width),
            vm(Z, prow, width),
            vm(width, width),
            vm(width, width),
            vm(width, 128),
            vm(hours, width),
            vm(hh, width),
            vm(hh, width),
            vm(hh, width),
            vm(Z, hh, width),
            vm(hours, width),
            vm(width, hours),
            vm(hours * NH, width),
            vm(width, points),
            vm(points, width),
            vm(Q, mrow, width),
            vm(brow, width),
            pltpu.VMEM((6 * STEP, width), bf16),
            pltpu.VMEM((6 * STEP, width), bf16),
            pltpu.SemaphoreType.DMA((hours + 2,)),
            pltpu.SemaphoreType.DMA((sems,)),
            pltpu.SemaphoreType.DMA((sems,)),
        ],
        compiler_params=pltpu.CompilerParams(
            collective_id=0,
            has_side_effects=True,
            vmem_limit_bytes=56 * 1024 * 1024,
        ),
    )(tensor, b_factor, c_factor)


def solution(mesh):
    sizes = (mesh.shape["pts"], mesh.shape["hrs"], mesh.shape["bins"])
    placed = (P("hrs", "pts", "bins"), P(("pts", "hrs"), None), P("bins", None))
    return jax.shard_map(
        functools.partial(local, sizes),
        mesh=mesh,
        in_specs=placed,
        out_specs=(P("hrs", None), P(("pts", "hrs"), None)),
        check_vma=False,
    )
```

```python
import functools

import jax
import jax.numpy as jnp
from jax import lax
from jax.experimental import pallas as pl
from jax.experimental.pallas import tpu as pltpu
from jax.sharding import PartitionSpec as P

f32 = jnp.float32
bf16 = jnp.bfloat16
HIGHEST = lax.Precision.HIGHEST
MESH = pl.DeviceIdType.MESH
CONTRACT_ROWS = (((0,), (0,)), ((), ()))


def dot(a, b, dims):
    return lax.dot_general(a, b, (dims, ((), ())), preferred_element_type=f32)


def halves(x):
    hi = x.astype(bf16)
    return hi, (x - hi.astype(f32)).astype(bf16)


def gram(x):
    hi = x.astype(bf16).astype(f32)
    lo = x - hi
    left = jnp.concatenate([hi, hi, lo, lo], axis=0).astype(bf16)
    right = jnp.concatenate([hi, lo, hi, lo], axis=0).astype(bf16)
    return dot(left, right, ((0,), (0,)))


def split(x):
    first = x.astype(bf16).astype(f32)
    rest = x - first
    second = rest.astype(bf16).astype(f32)
    return first, second, rest - second


STEP = 16


def spread_lanes(x, first):
    return [
        jnp.take_along_axis(
            x,
            jnp.full(x.shape, first + j, jnp.int32),
            axis=1,
            mode="promise_in_bounds",
        )
        for j in range(STEP)
    ]


def spread_row(x, j):
    return jnp.broadcast_to(x[j : j + 1, :], x.shape)


def lane_tile(x, t):
    return jnp.where(t == 0, x[:, :128], x[:, 128:])


def pivot(panel, row):
    lane = lax.broadcasted_iota(jnp.int32, panel.shape, 1)
    sub = lax.broadcasted_iota(jnp.int32, panel.shape, 0)
    rel = lane - row
    t = row // 128
    cols = spread_lanes(lane_tile(panel, t), row - t * 128)
    work = jnp.where((rel >= 0) & (rel < STEP), jnp.where(rel == sub, 1.0, 0.0), panel)
    data = [work[:, :128], work[:, 128:]]
    sub = lax.broadcasted_iota(jnp.int32, (STEP, 128), 0)
    for j in range(STEP):
        state = cols[j:] + data
        rows = [spread_row(x, j) for x in state]
        inverse = pltpu.reciprocal(rows[0], approx=False)
        factor = jnp.where(sub == j, 1.0 - inverse, cols[j] * inverse)
        state = [x - factor * r for x, r in zip(state, rows)]
        cols = cols[:j] + state[: STEP - j]
        data = state[STEP - j :]
    column = jnp.where(lane < row, -panel, panel)
    return jnp.concatenate(data, axis=1), column


def follow(rows, done, row):
    rel = lax.broadcasted_iota(jnp.int32, rows.shape, 1) - row
    t = row // 128
    cols = spread_lanes(lane_tile(rows, t), row - t * 128)
    rows = jnp.where((rel >= 0) & (rel < STEP), 0.0, rows)
    out = []
    for s in (0, 128):
        part = done[:, s : s + 128]
        terms = [cols[j] * spread_row(part, j) for j in range(STEP)]
        while len(terms) > 1:
            terms = [x + y for x, y in zip(terms[::2], terms[1::2])]
        out.append(rows[:, s : s + 128] - terms[0])
    return jnp.concatenate(out, axis=1)


def factors(left, right, column, done):
    c1, c2, c3 = split(column)
    r1, r2, r3 = split(done)
    left[...] = jnp.concatenate([c1, c1, c2, c2, c1, c3], axis=0).astype(bf16)
    right[...] = jnp.concatenate([r1, r2, r1, r2, r3, r1], axis=0).astype(bf16)


def late_update(a, left, right, row, done):
    update = lax.dot_general(
        left[...], right[...], CONTRACT_ROWS, preferred_element_type=f32
    )
    rel = lax.broadcasted_iota(jnp.int32, a.shape, 1) - row
    a[...] = jnp.where((rel >= 0) & (rel < STEP), 0.0, a[...]) - update
    a[pl.ds(row, STEP), :] = done


def invert(a, left, right, pauses):
    steps = a.shape[0] // STEP

    def at(k):
        return pl.multiple_of(k * STEP, STEP)

    done, column = pivot(a[0:STEP, :], 0)
    factors(left, right, column, done)
    panel = follow(a[STEP : 2 * STEP, :], done, 0)

    def body(k, carry):
        panel, before = carry
        late_update(a, left, right, at(k - 1), before)
        done, column = pivot(panel, at(k))
        panel = follow(a[pl.ds(at(k + 1), STEP), :], done, at(k))
        factors(left, right, column, done)
        return panel, done

    carry = (panel, done)
    first = 1
    for stop in sorted(pauses):
        carry = lax.fori_loop(first, stop, body, carry)
        pauses[stop]()
        first = stop
    panel, before = lax.fori_loop(first, steps - 1, body, carry)
    late_update(a, left, right, at(steps - 2), before)
    done, column = pivot(panel, at(steps - 1))
    factors(left, right, column, done)
    late_update(a, left, right, at(steps - 1), done)


def kernel(
    sizes,
    t_hbm,
    b_hbm,
    c_hbm,
    hf_ref,
    pf_ref,
    tbuf,
    con,
    cbuf,
    ct,
    bbuf,
    bx,
    bt,
    gb_part,
    gb_in,
    gb_z,
    gc_part,
    gc_in,
    hmat,
    gcm,
    mht,
    mh,
    mh_in,
    mh_z,
    mh_all,
    hft,
    hfall,
    mpt,
    mp,
    mp_in,
    owned,
    left,
    right,
    lsem,
    ssem,
    rsem,
):
    NP, NH, NB = sizes
    Z, Q, NX = NP // 2, NH * NB, NH // 2
    YC = 8
    hours, _, points = t_hbm.shape
    width = c_hbm.shape[1]
    half = width // 2
    prow = half // Q
    brow = b_hbm.shape[0]
    bhalf = brow // 2
    mrow = points // Q
    hh = hours // 2
    p, h, n = lax.axis_index("pts"), lax.axis_index("hrs"), lax.axis_index("bins")
    z, core = p // 2, lax.rem(p, 2)
    y_hi, x = h // NX, lax.rem(h, NX)
    q = h * NB + n
    w = (2 * y_hi + n) * 2 + core
    g = 2 * core + n

    def plane(d):
        t = lax.rem(q + d, Q)
        return (p, t // NB, lax.rem(t, NB))

    def along_x(d):
        return (p, y_hi * NX + lax.rem(x + d, NX), n)

    def hour_block(d):
        flip = d // NX
        return (
            p,
            lax.rem(y_hi + flip, 2) * NX + lax.rem(x + d, NX),
            lax.rem(n + flip, 2),
        )

    def along_z(d):
        return (lax.rem(z + d, Z) * 2 + core, h, n)

    def split_w(d):
        t = lax.rem(w + d, YC)
        return t // 4, lax.rem(t // 2, 2), lax.rem(t, 2)

    def column(d):
        y2, n2, core2 = split_w(d)
        return (z * 2 + core2, y2 * NX + x, n2)

    def quad(d):
        t = lax.rem(g + d, 4)
        return (z * 2 + t // 2, h, lax.rem(t, 2))

    other_core = (p + 1 - 2 * core, h, n)
    other_bins = (p, h, 1 - n)

    def remote(src, dst, i, target):
        return pltpu.make_async_remote_copy(
            src_ref=src,
            dst_ref=dst,
            send_sem=ssem.at[i],
            recv_sem=rsem.at[i],
            device_id=target,
            device_id_type=MESH,
        )

    def start_all(count, make, first=1):
        def body(d, _):
            make(d).start()
            return 0

        lax.fori_loop(first, count, body, 0)

    def wait_all(count, make, first=1):
        def body(d, _):
            make(d).wait()
            return 0

        lax.fori_loop(first, count, body, 0)

    def at(i, size):
        return pl.ds(pl.multiple_of(i * size, 8), size)

    base = 0

    def take(count):
        nonlocal base
        base += count
        return base - count

    my_b = at(h, brow)
    load_b = pltpu.make_async_copy(b_hbm, bbuf.at[my_b], lsem.at[hours])
    load_c = pltpu.make_async_copy(c_hbm, cbuf, lsem.at[hours + 1])
    load_b.start()
    load_c.start()

    def load_t(i):
        return pltpu.make_async_copy(t_hbm.at[i], tbuf.at[i], lsem.at[i])

    def start_t(i, _):
        load_t(i).start()
        return 0

    lax.fori_loop(0, hours, start_t, 0)

    barrier = pltpu.get_barrier_semaphore()

    def greet(make):
        def body(d, _):
            pl.semaphore_signal(
                barrier, inc=1, device_id=make(d), device_id_type=MESH
            )
            return 0

        return body

    lax.fori_loop(1, Q, greet(plane), 0)
    lax.fori_loop(1, Z, greet(along_z), 0)

    def greet_column(i, _):
        pl.semaphore_signal(
            barrier,
            inc=1,
            device_id=(z * 2 + 1 - core, (i // 2) * NX + x, lax.rem(i, 2)),
            device_id_type=MESH,
        )
        return 0

    lax.fori_loop(0, YC // 2, greet_column, 0)
    pl.semaphore_wait(barrier, Q - 1 + Z - 1 + YC // 2)

    load_b.wait()
    bx[at(x, bhalf), :] = bbuf[pl.ds(pl.multiple_of(h * brow + n * bhalf, 8), bhalf), :]
    x_base = take(NX)
    send_x = lambda d: remote(
        bx.at[at(x, bhalf)], bx.at[at(x, bhalf)], x_base + d, along_x(d)
    )
    start_all(NX, send_x)

    load_c.wait()
    chi, clo = halves(cbuf[...].T)
    ct[:width, :] = chi
    ct[width:, :] = clo

    def contract(i, _):
        load_t(i).wait()
        thi, tlo = halves(tbuf[i])
        chi, clo = ct[:width, :], ct[width:, :]
        mul = functools.partial(dot, dims=((1,), (0,)))
        con[i] = mul(chi, thi) + (mul(clo, thi) + mul(chi, tlo))
        return 0

    def contract_hours(first, last):
        lax.fori_loop(first * hours // 16, last * hours // 16, contract, 0)

    contract_hours(0, 1)

    wait_all(NX, send_x)
    gb_part[...] = gram(bx[...])
    my_rows = pl.ds(pl.multiple_of(half * core + prow * q, 8), prow)
    col_base = take(YC)

    def send_col(d):
        y2, n2, core2 = split_w(d)
        q2 = (y2 * NX + x) * NB + n2
        rows = pl.ds(pl.multiple_of(half * core2 + prow * q2, 8), prow)
        return remote(gb_part.at[rows], gb_in.at[w], col_base + d, column(d))

    start_all(YC, send_col)
    gb_in[w] = gb_part[my_rows, :]

    chi, clo = ct[:width, :], ct[width:, :]
    mul = functools.partial(dot, dims=((1,), (1,)))
    gc_part[...] = mul(chi, chi) + (mul(chi, clo) + mul(clo, chi))
    bins_rows = pl.ds(
        pl.multiple_of(half * core + prow * (h * NB + 1 - n), 8), prow
    )
    send_gc = remote(gc_part.at[bins_rows], gc_in, take(1), other_bins)
    send_gc.start()
    contract_hours(1, 3)

    def add_up(ref, count):
        total = ref[0]
        for s in range(1, count):
            total = total + ref[s]
        return total

    wait_all(YC, send_col)
    gb_z[z] = add_up(gb_in, YC)
    z_base = take(Z)
    send_gbz = lambda d: remote(gb_z.at[z], gb_z.at[z], z_base + d, along_z(d))
    start_all(Z, send_gbz)
    contract_hours(3, 7)

    wait_all(Z, send_gbz)
    send_gc.wait()
    gcm[my_rows, :] = gc_part[my_rows, :] + gc_in[...]
    hmat[my_rows, :] = add_up(gb_z, Z) * gcm[my_rows, :]
    h_base = take(Q)
    send_h = lambda d: remote(hmat.at[my_rows], hmat.at[my_rows], h_base + d, plane(d))
    start_all(Q, send_h)

    bx_base = take(NX)
    b_other = pl.ds(pl.multiple_of(h * brow + (1 - n) * bhalf, 8), bhalf)
    send_b2 = lambda d: remote(
        bbuf.at[b_other], bbuf.at[b_other], bx_base + d, along_x(d)
    )
    b_base = take(NH)
    send_b = lambda d: remote(bbuf.at[my_b], bbuf.at[my_b], b_base + d, hour_block(d))
    start_all(NX, send_b2)
    start_all(NH, send_b, NX)
    contract_hours(7, 13)

    wait_all(Q, send_h)
    my_half = at(core, half)
    swap_h = remote(hmat.at[my_half], hmat.at[my_half], take(1), other_core)
    swap_h.start()
    gc_base = take(Q)
    send_gcm = lambda d: remote(
        gcm.at[my_rows], gcm.at[my_rows], gc_base + d, plane(d)
    )
    start_all(Q, send_gcm)
    contract_hours(13, 16)

    wait_all(NX, send_b2)
    wait_all(NH, send_b, NX)

    def own_rows(d, _):
        rows = pl.ds(
            pl.multiple_of((y_hi * NX + d) * brow + n * bhalf, 8), bhalf
        )
        bbuf[rows, :] = bx[at(d, bhalf), :]
        return 0

    lax.fori_loop(0, NX, own_rows, 0)
    bt[...] = bbuf[...].T
    lane = lax.broadcasted_iota(jnp.int32, mht.shape, 1)

    def partial_hours(i, _):
        total = jnp.sum(con[i] * bt[...], axis=1, keepdims=True)
        mht[...] = jnp.where(lane == i, total, mht[...])
        return 0

    lax.fori_loop(0, hours, partial_hours, 0)
    mh[...] = mht[...].T[:hours, :]

    def tile(c2, n2):
        return at(c2, hh), pl.ds(pl.multiple_of(n2 * half, 128), half)

    my_tile = tile(core, n)
    mq_base = take(4)

    def send_mq(d):
        t = lax.rem(g + d, 4)
        return remote(
            mh.at[tile(t // 2, lax.rem(t, 2))], mh_in.at[g], mq_base + d, quad(d)
        )

    start_all(4, send_mq)
    mh_in[g] = mh[my_tile]
    mz_base = take(Z)
    send_mz = lambda d: remote(mh_z.at[z], mh_z.at[z], mz_base + d, along_z(d))
    ma_base = take(4)
    send_ma = lambda d: remote(
        mh_all.at[my_tile], mh_all.at[my_tile], ma_base + d, quad(d)
    )

    def pause_quad():
        wait_all(4, send_mq)
        mh_z[z] = add_up(mh_in, 4)
        start_all(Z, send_mz)

    def pause_z():
        wait_all(Z, send_mz)
        mh_all[my_tile] = add_up(mh_z, Z)
        start_all(4, send_ma)

    swap_h.wait()
    invert(hmat, left, right, {4: pause_quad, 9: pause_z})
    wait_all(4, send_ma)
    wait_all(Q, send_gcm)
    swap_gc = remote(gcm.at[my_half], gcm.at[my_half], take(1), other_core)

    hf = jnp.dot(
        mh_all[...], hmat[...], precision=HIGHEST, preferred_element_type=f32
    )
    my_hours = at(h, hours)
    hfall[my_hours, :] = hf
    hf_base = take(NH)
    send_hf = lambda d: remote(
        hfall.at[my_hours], hfall.at[my_hours], hf_base + d, hour_block(d)
    )
    start_all(NH, send_hf)
    swap_gc.start()
    hft[...] = hf.T
    hf_ref[...] = hf

    chunk = 32
    for rows in range(0, width, chunk):
        weights = hft[rows : rows + chunk, :]
        acc = con[0, rows : rows + chunk, :] * weights[:, 0:1]
        for i in range(1, hours):
            acc = acc + con[i, rows : rows + chunk, :] * weights[:, i : i + 1]
        mpt[rows : rows + chunk, :] = acc
    mp[...] = mpt[...].T
    mp_base = take(Q)

    def send_mp(d):
        t = lax.rem(q + d, Q)
        return remote(mp.at[at(t, mrow)], mp_in.at[d], mp_base + d, plane(d))

    start_all(Q, send_mp)

    wait_all(NH, send_hf)
    swap_gc.wait()
    hmat[...] = gram(hfall[...]) * gcm[...]
    mine = at(n, mrow)
    swap_o = remote(owned.at[mine], owned.at[mine], take(1), other_bins)

    def pause_points():
        wait_all(Q, send_mp)
        total = mp[at(q, mrow), :]
        for s in range(1, Q):
            total = total + mp_in[s]
        owned[mine, :] = total
        swap_o.start()

    invert(hmat, left, right, {8: pause_points})
    swap_o.wait()
    pf_ref[...] = jnp.dot(
        owned[...], hmat[...], precision=HIGHEST, preferred_element_type=f32
    )


def local(sizes, tensor, b_factor, c_factor):
    NP, NH, NB = sizes
    Z, Q, NX = NP // 2, NH * NB, NH // 2
    tensor = jnp.swapaxes(tensor, 1, 2)
    hours, bins, points = tensor.shape
    width = c_factor.shape[1]
    brow = b_factor.shape[0]
    prow = width // (2 * Q)
    mrow = points // Q
    hh = hours // 2
    YC = 8
    sems = 2 * NX + YC + 1 + 2 * Z + 3 * Q + 2 * NH + 11
    vm = lambda *shape: pltpu.VMEM(shape, f32)
    any_spec = pl.BlockSpec(memory_space=pltpu.HBM)
    vmem_spec = pl.BlockSpec(memory_space=pltpu.VMEM)
    return pl.pallas_call(
        functools.partial(kernel, sizes),
        out_shape=(
            jax.ShapeDtypeStruct((hours, width), f32),
            jax.ShapeDtypeStruct((brow, width), f32),
        ),
        in_specs=[any_spec] * 3,
        out_specs=(vmem_spec, vmem_spec),
        scratch_shapes=[
            vm(hours, bins, points),
            vm(hours, width, points),
            vm(bins, width),
            pltpu.VMEM((2 * width, bins), bf16),
            vm(points, width),
            vm(NX * brow // 2, width),
            vm(width, points),
            vm(width, width),
            vm(YC, prow, width),
            vm(Z, prow, width),
            vm(width, width),
            vm(prow, width),
            vm(width, width),
            vm(width, width),
            vm(width, 128),
            vm(hours, width),
            vm(4, hh, width // 2),
            vm(Z, hh, width // 2),
            vm(hours, width),
            vm(width, hours),
            vm(hours * NH, width),
            vm(width, points),
            vm(points, width),
            vm(Q, mrow, width),
            vm(brow, width),
            pltpu.VMEM((6 * STEP, width), bf16),
            pltpu.VMEM((6 * STEP, width), bf16),
            pltpu.SemaphoreType.DMA((hours + 2,)),
            pltpu.SemaphoreType.DMA((sems,)),
            pltpu.SemaphoreType.DMA((sems,)),
        ],
        compiler_params=pltpu.CompilerParams(
            collective_id=0,
            has_side_effects=True,
            vmem_limit_bytes=56 * 1024 * 1024,
        ),
    )(tensor, b_factor, c_factor)


def solution(mesh):
    sizes = (mesh.shape["pts"], mesh.shape["hrs"], mesh.shape["bins"])
    placed = (P("hrs", "pts", "bins"), P(("pts", "hrs"), None), P("bins", None))
    return jax.shard_map(
        functools.partial(local, sizes),
        mesh=mesh,
        in_specs=placed,
        out_specs=(P("hrs", None), P(("pts", "hrs"), None)),
        check_vma=False,
    )
```

```python
import functools

import jax
import jax.numpy as jnp
from jax import lax
from jax.experimental import pallas as pl
from jax.experimental.pallas import tpu as pltpu
from jax.sharding import PartitionSpec as P

f32 = jnp.float32
bf16 = jnp.bfloat16
HIGHEST = lax.Precision.HIGHEST
MESH = pl.DeviceIdType.MESH
CONTRACT_ROWS = (((0,), (0,)), ((), ()))


def dot(a, b, dims):
    return lax.dot_general(a, b, (dims, ((), ())), preferred_element_type=f32)


def halves(x):
    hi = x.astype(bf16)
    return hi, (x - hi.astype(f32)).astype(bf16)


def gram(x):
    hi = x.astype(bf16).astype(f32)
    lo = x - hi
    left = jnp.concatenate([hi, hi, lo, lo], axis=0).astype(bf16)
    right = jnp.concatenate([hi, lo, hi, lo], axis=0).astype(bf16)
    return dot(left, right, ((0,), (0,)))


def split(x):
    first = x.astype(bf16).astype(f32)
    rest = x - first
    second = rest.astype(bf16).astype(f32)
    return first, second, rest - second


STEP = 16


def spread_lanes(x, first):
    return [
        jnp.take_along_axis(
            x,
            jnp.full(x.shape, first + j, jnp.int32),
            axis=1,
            mode="promise_in_bounds",
        )
        for j in range(STEP)
    ]


def spread_row(x, j):
    return jnp.broadcast_to(x[j : j + 1, :], x.shape)


def lane_tile(x, t):
    return jnp.where(t == 0, x[:, :128], x[:, 128:])


def pivot(panel, row):
    lane = lax.broadcasted_iota(jnp.int32, panel.shape, 1)
    sub = lax.broadcasted_iota(jnp.int32, panel.shape, 0)
    rel = lane - row
    t = row // 128
    cols = spread_lanes(lane_tile(panel, t), row - t * 128)
    work = jnp.where((rel >= 0) & (rel < STEP), jnp.where(rel == sub, 1.0, 0.0), panel)
    data = [work[:, :128], work[:, 128:]]
    sub = lax.broadcasted_iota(jnp.int32, (STEP, 128), 0)
    for j in range(STEP):
        state = cols[j:] + data
        rows = [spread_row(x, j) for x in state]
        inverse = pltpu.reciprocal(rows[0], approx=False)
        factor = jnp.where(sub == j, 1.0 - inverse, cols[j] * inverse)
        state = [x - factor * r for x, r in zip(state, rows)]
        cols = cols[:j] + state[: STEP - j]
        data = state[STEP - j :]
    column = jnp.where(lane < row, -panel, panel)
    return jnp.concatenate(data, axis=1), column


def follow(rows, done, row):
    rel = lax.broadcasted_iota(jnp.int32, rows.shape, 1) - row
    t = row // 128
    cols = spread_lanes(lane_tile(rows, t), row - t * 128)
    rows = jnp.where((rel >= 0) & (rel < STEP), 0.0, rows)
    out = []
    for s in (0, 128):
        part = done[:, s : s + 128]
        terms = [cols[j] * spread_row(part, j) for j in range(STEP)]
        while len(terms) > 1:
            terms = [x + y for x, y in zip(terms[::2], terms[1::2])]
        out.append(rows[:, s : s + 128] - terms[0])
    return jnp.concatenate(out, axis=1)


def factors(left, right, column, done):
    c1, c2, c3 = split(column)
    r1, r2, r3 = split(done)
    left[...] = jnp.concatenate([c1, c1, c2, c2, c1, c3], axis=0).astype(bf16)
    right[...] = jnp.concatenate([r1, r2, r1, r2, r3, r1], axis=0).astype(bf16)


def late_update(a, left, right, row, done):
    update = lax.dot_general(
        left[...], right[...], CONTRACT_ROWS, preferred_element_type=f32
    )
    rel = lax.broadcasted_iota(jnp.int32, a.shape, 1) - row
    a[...] = jnp.where((rel >= 0) & (rel < STEP), 0.0, a[...]) - update
    a[pl.ds(row, STEP), :] = done


def invert(a, left, right, pauses):
    steps = a.shape[0] // STEP

    def at(k):
        return pl.multiple_of(k * STEP, STEP)

    done, column = pivot(a[0:STEP, :], 0)
    factors(left, right, column, done)
    panel = follow(a[STEP : 2 * STEP, :], done, 0)

    def body(k, carry):
        panel, before = carry
        late_update(a, left, right, at(k - 1), before)
        done, column = pivot(panel, at(k))
        panel = follow(a[pl.ds(at(k + 1), STEP), :], done, at(k))
        factors(left, right, column, done)
        return panel, done

    carry = (panel, done)
    first = 1
    for stop in sorted(pauses):
        carry = lax.fori_loop(first, stop, body, carry)
        pauses[stop]()
        first = stop
    panel, before = lax.fori_loop(first, steps - 1, body, carry)
    late_update(a, left, right, at(steps - 2), before)
    done, column = pivot(panel, at(steps - 1))
    factors(left, right, column, done)
    late_update(a, left, right, at(steps - 1), done)


def kernel(
    sizes,
    t_hbm,
    b_hbm,
    c_hbm,
    hf_ref,
    pf_ref,
    tbuf,
    con,
    cbuf,
    ct,
    bbuf,
    bx,
    bt,
    gb_part,
    gb_in,
    gb_z,
    gc_part,
    gc_in,
    hmat,
    gcm,
    mht,
    mh,
    mh_in,
    mh_z,
    mhall,
    hft,
    hfall,
    mpt,
    mp,
    mp_in,
    owned,
    owned_in,
    left,
    right,
    lsem,
    ssem,
    rsem,
):
    NP, NH, NB = sizes
    Z, Q, NX = NP // 2, NH * NB, NH // 2
    YC = 8
    COL = (3, 8)
    hours, _, points = t_hbm.shape
    width = c_hbm.shape[1]
    half = width // 2
    prow = half // Q
    brow = b_hbm.shape[0]
    bhalf = brow // 2
    mrow = points // Q
    hh = hours // 2
    p, h, n = lax.axis_index("pts"), lax.axis_index("hrs"), lax.axis_index("bins")
    z, core = p // 2, lax.rem(p, 2)
    y_hi, x = h // NX, lax.rem(h, NX)
    q = h * NB + n
    w = (2 * y_hi + n) * 2 + core
    g = 2 * core + n

    def plane(d):
        t = lax.rem(q + d, Q)
        return (p, t // NB, lax.rem(t, NB))

    def along_x(d):
        return (p, y_hi * NX + lax.rem(x + d, NX), n)

    def hour_block(d):
        flip = d // NX
        return (
            p,
            lax.rem(y_hi + flip, 2) * NX + lax.rem(x + d, NX),
            lax.rem(n + flip, 2),
        )

    def along_z(d):
        return (lax.rem(z + d, Z) * 2 + core, h, n)

    def split_w(d):
        t = lax.rem(w + d, YC)
        return t // 4, lax.rem(t // 2, 2), lax.rem(t, 2)

    def column(d):
        y2, n2, core2 = split_w(d)
        return (z * 2 + core2, y2 * NX + x, n2)

    def quad(d):
        t = lax.rem(g + d, 4)
        return (z * 2 + t // 2, h, lax.rem(t, 2))

    other_core = (p + 1 - 2 * core, h, n)
    other_bins = (p, h, 1 - n)

    def remote(src, dst, i, target):
        return pltpu.make_async_remote_copy(
            src_ref=src,
            dst_ref=dst,
            send_sem=ssem.at[i],
            recv_sem=rsem.at[i],
            device_id=target,
            device_id_type=MESH,
        )

    def start_all(count, make, first=1):
        def body(d, _):
            make(d).start()
            return 0

        lax.fori_loop(first, count, body, 0)

    def wait_all(count, make, first=1):
        def body(d, _):
            make(d).wait()
            return 0

        lax.fori_loop(first, count, body, 0)

    def at(i, size):
        return pl.ds(pl.multiple_of(i * size, 8), size)

    base = 0

    def take(count):
        nonlocal base
        base += count
        return base - count

    my_b = at(h, brow)
    load_b = pltpu.make_async_copy(b_hbm, bbuf.at[my_b], lsem.at[hours])
    load_c = pltpu.make_async_copy(c_hbm, cbuf, lsem.at[hours + 1])
    load_b.start()
    load_c.start()

    def load_t(i):
        return pltpu.make_async_copy(t_hbm.at[i], tbuf.at[i], lsem.at[i])

    def start_t(i, _):
        load_t(i).start()
        return 0

    lax.fori_loop(0, hours, start_t, 0)

    barrier = pltpu.get_barrier_semaphore()

    def greet(make):
        def body(d, _):
            pl.semaphore_signal(
                barrier, inc=1, device_id=make(d), device_id_type=MESH
            )
            return 0

        return body

    lax.fori_loop(1, Q, greet(plane), 0)
    lax.fori_loop(1, Z, greet(along_z), 0)

    def greet_column(i, _):
        pl.semaphore_signal(
            barrier,
            inc=1,
            device_id=(z * 2 + 1 - core, (i // 2) * NX + x, lax.rem(i, 2)),
            device_id_type=MESH,
        )
        return 0

    lax.fori_loop(0, YC // 2, greet_column, 0)
    pl.semaphore_wait(barrier, Q - 1 + Z - 1 + YC // 2)

    load_b.wait()
    bx[at(x, bhalf), :] = bbuf[pl.ds(pl.multiple_of(h * brow + n * bhalf, 8), bhalf), :]
    x_base = take(NX)
    send_x = lambda d: remote(
        bx.at[at(x, bhalf)], bx.at[at(x, bhalf)], x_base + d, along_x(d)
    )
    start_all(NX, send_x)

    load_c.wait()
    chi, clo = halves(cbuf[...].T)
    ct[:width, :] = chi
    ct[width:, :] = clo

    def contract(i, _):
        load_t(i).wait()
        thi, tlo = halves(tbuf[i])
        chi, clo = ct[:width, :], ct[width:, :]
        mul = functools.partial(dot, dims=((1,), (0,)))
        con[i] = mul(chi, thi) + (mul(clo, thi) + mul(chi, tlo))
        return 0

    def contract_hours(first, last):
        lax.fori_loop(first * hours // 16, last * hours // 16, contract, 0)

    contract_hours(0, COL[0])

    wait_all(NX, send_x)
    gb_part[...] = gram(bx[...])
    my_rows = pl.ds(pl.multiple_of(half * core + prow * q, 8), prow)
    col_base = take(YC)

    def send_col(d):
        y2, n2, core2 = split_w(d)
        q2 = (y2 * NX + x) * NB + n2
        rows = pl.ds(pl.multiple_of(half * core2 + prow * q2, 8), prow)
        return remote(gb_part.at[rows], gb_in.at[w], col_base + d, column(d))

    start_all(YC, send_col)
    gb_in[w] = gb_part[my_rows, :]

    bx_base = take(NX)
    b_other = pl.ds(pl.multiple_of(h * brow + (1 - n) * bhalf, 8), bhalf)
    send_b2 = lambda d: remote(
        bbuf.at[b_other], bbuf.at[b_other], bx_base + d, along_x(d)
    )
    b_base = take(NH)
    send_b = lambda d: remote(bbuf.at[my_b], bbuf.at[my_b], b_base + d, hour_block(d))
    start_all(NX, send_b2)
    start_all(NH, send_b, NX)

    chi, clo = ct[:width, :], ct[width:, :]
    mul = functools.partial(dot, dims=((1,), (1,)))
    gc_part[...] = mul(chi, chi) + (mul(chi, clo) + mul(clo, chi))
    my_half = at(core, half)
    send_gc = remote(gc_part.at[my_half], gc_in, take(1), other_bins)
    send_gc.start()
    contract_hours(COL[0], COL[1])

    def add_up(ref, count):
        total = ref[0]
        for s in range(1, count):
            total = total + ref[s]
        return total

    wait_all(YC, send_col)
    gb_z[z] = add_up(gb_in, YC)
    z_base = take(Z)
    send_gbz = lambda d: remote(gb_z.at[z], gb_z.at[z], z_base + d, along_z(d))
    start_all(Z, send_gbz)
    contract_hours(COL[1], 16)

    wait_all(NX, send_b2)
    wait_all(NH, send_b, NX)

    def own_rows(d, _):
        rows = pl.ds(
            pl.multiple_of((y_hi * NX + d) * brow + n * bhalf, 8), bhalf
        )
        bbuf[rows, :] = bx[at(d, bhalf), :]
        return 0

    lax.fori_loop(0, NX, own_rows, 0)
    bt[...] = bbuf[...].T
    lane = lax.broadcasted_iota(jnp.int32, mht.shape, 1)

    def partial_hours(i, _):
        total = jnp.sum(con[i] * bt[...], axis=1, keepdims=True)
        mht[...] = jnp.where(lane == i, total, mht[...])
        return 0

    lax.fori_loop(0, hours, partial_hours, 0)
    mh[...] = mht[...].T[:hours, :]

    def tile(c2, n2):
        return at(c2, hh), pl.ds(pl.multiple_of(n2 * half, 128), half)

    my_tile = tile(core, n)
    mq_base = take(4)

    def send_mq(d):
        t = lax.rem(g + d, 4)
        return remote(
            mh.at[tile(t // 2, lax.rem(t, 2))], mh_in.at[g], mq_base + d, quad(d)
        )

    start_all(4, send_mq)
    mh_in[g] = mh[my_tile]
    mz_base = take(Z)
    send_mz = lambda d: remote(mh_z.at[z], mh_z.at[z], mz_base + d, along_z(d))
    my_hours = at(h, hours)
    ma_base = take(4)
    my_part = (
        pl.ds(pl.multiple_of(h * hours + core * hh, 8), hh),
        pl.ds(pl.multiple_of(n * half, 128), half),
    )
    send_ma = lambda d: remote(
        mhall.at[my_part], mhall.at[my_part], ma_base + d, quad(d)
    )
    mr_base = take(NH)
    send_mr = lambda d: remote(
        mhall.at[my_hours], mhall.at[my_hours], mr_base + d, hour_block(d)
    )

    wait_all(Z, send_gbz)
    send_gc.wait()
    gcm[my_half, :] = gc_part[my_half, :] + gc_in[...]
    swap_gc = remote(gcm.at[my_half], gcm.at[my_half], take(1), other_core)
    hmat[my_rows, :] = add_up(gb_z, Z) * gcm[my_rows, :]
    h_base = take(Q)
    send_h = lambda d: remote(hmat.at[my_rows], hmat.at[my_rows], h_base + d, plane(d))
    start_all(Q, send_h)
    swap_gc.start()

    wait_all(4, send_mq)
    mh_z[z] = add_up(mh_in, 4)
    start_all(Z, send_mz)

    wait_all(Q, send_h)
    swap_h = remote(hmat.at[my_half], hmat.at[my_half], take(1), other_core)
    swap_h.start()

    def pause_z():
        wait_all(Z, send_mz)
        mhall[my_part] = add_up(mh_z, Z)
        start_all(4, send_ma)

    def pause_quad():
        wait_all(4, send_ma)
        start_all(NH, send_mr)

    swap_h.wait()
    invert(hmat, left, right, {3: pause_z, 9: pause_quad})
    wait_all(NH, send_mr)
    swap_gc.wait()

    hfall[...] = jnp.dot(
        mhall[...], hmat[...], precision=HIGHEST, preferred_element_type=f32
    )
    hf = hfall[my_hours, :]
    hft[...] = hf.T
    hf_ref[...] = hf

    chunk = 32
    for rows in range(0, width, chunk):
        weights = hft[rows : rows + chunk, :]
        acc = con[0, rows : rows + chunk, :] * weights[:, 0:1]
        for i in range(1, hours):
            acc = acc + con[i, rows : rows + chunk, :] * weights[:, i : i + 1]
        mpt[rows : rows + chunk, :] = acc
    mp[...] = mpt[...].T
    mp_base = take(NH)

    def send_mp(d):
        flip = d // NX
        h2 = lax.rem(y_hi + flip, 2) * NX + lax.rem(x + d, NX)
        return remote(mp.at[at(h2, brow)], mp_in.at[d], mp_base + d, hour_block(d))

    start_all(NH, send_mp)
    hmat[...] = gram(hfall[...]) * gcm[...]
    swap_o = remote(owned, owned_in, take(1), other_bins)

    def pause_points():
        wait_all(NH, send_mp)
        total = mp[my_b, :]
        for s in range(1, NH):
            total = total + mp_in[s]
        owned[...] = total
        swap_o.start()

    invert(hmat, left, right, {13: pause_points})
    swap_o.wait()
    pf_ref[...] = jnp.dot(
        owned[...] + owned_in[...],
        hmat[...],
        precision=HIGHEST,
        preferred_element_type=f32,
    )


def local(sizes, tensor, b_factor, c_factor):
    NP, NH, NB = sizes
    Z, Q, NX = NP // 2, NH * NB, NH // 2
    tensor = jnp.swapaxes(tensor, 1, 2)
    hours, bins, points = tensor.shape
    width = c_factor.shape[1]
    brow = b_factor.shape[0]
    prow = width // (2 * Q)
    mrow = points // Q
    hh = hours // 2
    YC = 8
    sems = 2 * NX + YC + 1 + 2 * Z + 3 * Q + 2 * NH + 11
    vm = lambda *shape: pltpu.VMEM(shape, f32)
    any_spec = pl.BlockSpec(memory_space=pltpu.HBM)
    vmem_spec = pl.BlockSpec(memory_space=pltpu.VMEM)
    return pl.pallas_call(
        functools.partial(kernel, sizes),
        out_shape=(
            jax.ShapeDtypeStruct((hours, width), f32),
            jax.ShapeDtypeStruct((brow, width), f32),
        ),
        in_specs=[any_spec] * 3,
        out_specs=(vmem_spec, vmem_spec),
        scratch_shapes=[
            vm(hours, bins, points),
            vm(hours, width, points),
            vm(bins, width),
            pltpu.VMEM((2 * width, bins), bf16),
            vm(points, width),
            vm(NX * brow // 2, width),
            vm(width, points),
            vm(width, width),
            vm(YC, prow, width),
            vm(Z, prow, width),
            vm(width, width),
            vm(width // 2, width),
            vm(width, width),
            vm(width, width),
            vm(width, 128),
            vm(hours, width),
            vm(4, hh, width // 2),
            vm(Z, hh, width // 2),
            vm(hours * NH, width),
            vm(width, hours),
            vm(hours * NH, width),
            vm(width, points),
            vm(points, width),
            vm(NH, brow, width),
            vm(brow, width),
            vm(brow, width),
            pltpu.VMEM((6 * STEP, width), bf16),
            pltpu.VMEM((6 * STEP, width), bf16),
            pltpu.SemaphoreType.DMA((hours + 2,)),
            pltpu.SemaphoreType.DMA((sems,)),
            pltpu.SemaphoreType.DMA((sems,)),
        ],
        compiler_params=pltpu.CompilerParams(
            collective_id=0,
            has_side_effects=True,
            vmem_limit_bytes=56 * 1024 * 1024,
        ),
    )(tensor, b_factor, c_factor)


def solution(mesh):
    sizes = (mesh.shape["pts"], mesh.shape["hrs"], mesh.shape["bins"])
    placed = (P("hrs", "pts", "bins"), P(("pts", "hrs"), None), P("bins", None))
    return jax.shard_map(
        functools.partial(local, sizes),
        mesh=mesh,
        in_specs=placed,
        out_specs=(P("hrs", None), P(("pts", "hrs"), None)),
        check_vma=False,
    )
```

```python
import functools

import jax
import jax.numpy as jnp
from jax import lax
from jax.experimental import pallas as pl
from jax.experimental.pallas import tpu as pltpu
from jax.sharding import PartitionSpec as P

f32 = jnp.float32
bf16 = jnp.bfloat16
HIGHEST = lax.Precision.HIGHEST
MESH = pl.DeviceIdType.MESH
CONTRACT_ROWS = (((0,), (0,)), ((), ()))


def dot(a, b, dims):
    return lax.dot_general(a, b, (dims, ((), ())), preferred_element_type=f32)


def halves(x):
    hi = x.astype(bf16)
    return hi, (x - hi.astype(f32)).astype(bf16)


def gram(x):
    hi = x.astype(bf16).astype(f32)
    lo = x - hi
    left = jnp.concatenate([hi, hi, lo], axis=0).astype(bf16)
    right = jnp.concatenate([hi, lo, hi], axis=0).astype(bf16)
    return dot(left, right, ((0,), (0,)))


def split(x):
    first = x.astype(bf16).astype(f32)
    rest = x - first
    second = rest.astype(bf16).astype(f32)
    return first, second, rest - second


STEP = 16


def spread_lanes(x, first):
    return [
        jnp.take_along_axis(
            x,
            jnp.full(x.shape, first + j, jnp.int32),
            axis=1,
            mode="promise_in_bounds",
        )
        for j in range(STEP)
    ]


def spread_row(x, j):
    return jnp.broadcast_to(x[j : j + 1, :], x.shape)


def lane_tile(x, t):
    return jnp.where(t == 0, x[:, :128], x[:, 128:])


def pivot(panel, row):
    lane = lax.broadcasted_iota(jnp.int32, panel.shape, 1)
    sub = lax.broadcasted_iota(jnp.int32, panel.shape, 0)
    rel = lane - row
    t = row // 128
    cols = spread_lanes(lane_tile(panel, t), row - t * 128)
    work = jnp.where((rel >= 0) & (rel < STEP), jnp.where(rel == sub, 1.0, 0.0), panel)
    data = [work[:, :128], work[:, 128:]]
    sub = lax.broadcasted_iota(jnp.int32, (STEP, 128), 0)
    for j in range(STEP):
        state = cols[j:] + data
        rows = [spread_row(x, j) for x in state]
        inverse = pltpu.reciprocal(rows[0], approx=False)
        factor = jnp.where(sub == j, 1.0 - inverse, cols[j] * inverse)
        state = [x - factor * r for x, r in zip(state, rows)]
        cols = cols[:j] + state[: STEP - j]
        data = state[STEP - j :]
    column = jnp.where(lane < row, -panel, panel)
    return jnp.concatenate(data, axis=1), column


def follow(rows, done, row):
    rel = lax.broadcasted_iota(jnp.int32, rows.shape, 1) - row
    t = row // 128
    cols = spread_lanes(lane_tile(rows, t), row - t * 128)
    rows = jnp.where((rel >= 0) & (rel < STEP), 0.0, rows)
    out = []
    for s in (0, 128):
        part = done[:, s : s + 128]
        terms = [cols[j] * spread_row(part, j) for j in range(STEP)]
        while len(terms) > 1:
            terms = [x + y for x, y in zip(terms[::2], terms[1::2])]
        out.append(rows[:, s : s + 128] - terms[0])
    return jnp.concatenate(out, axis=1)


def factors(left, right, column, done):
    c1, c2, c3 = split(column)
    r1, r2, r3 = split(done)
    left[...] = jnp.concatenate([c1, c1, c2, c2, c1, c3], axis=0).astype(bf16)
    right[...] = jnp.concatenate([r1, r2, r1, r2, r3, r1], axis=0).astype(bf16)


def late_update(a, left, right, row, done):
    update = lax.dot_general(
        left[...], right[...], CONTRACT_ROWS, preferred_element_type=f32
    )
    rel = lax.broadcasted_iota(jnp.int32, a.shape, 1) - row
    a[...] = jnp.where((rel >= 0) & (rel < STEP), 0.0, a[...]) - update
    a[pl.ds(row, STEP), :] = done


def invert(a, left, right, pauses):
    steps = a.shape[0] // STEP

    def at(k):
        return pl.multiple_of(k * STEP, STEP)

    done, column = pivot(a[0:STEP, :], 0)
    factors(left, right, column, done)
    panel = follow(a[STEP : 2 * STEP, :], done, 0)

    def body(k, carry):
        panel, before = carry
        late_update(a, left, right, at(k - 1), before)
        done, column = pivot(panel, at(k))
        panel = follow(a[pl.ds(at(k + 1), STEP), :], done, at(k))
        factors(left, right, column, done)
        return panel, done

    carry = (panel, done)
    first = 1
    for stop in sorted(pauses):
        carry = lax.fori_loop(first, stop, body, carry)
        pauses[stop]()
        first = stop
    panel, before = lax.fori_loop(first, steps - 1, body, carry)
    late_update(a, left, right, at(steps - 2), before)
    done, column = pivot(panel, at(steps - 1))
    factors(left, right, column, done)
    late_update(a, left, right, at(steps - 1), done)


def kernel(
    sizes,
    t_hbm,
    b_hbm,
    c_hbm,
    hf_ref,
    pf_ref,
    tbuf,
    con,
    cbuf,
    ct,
    bbuf,
    bt,
    gb_part,
    gb_in,
    gb_z,
    gc_part,
    gc_in,
    hmat,
    gcm,
    mht,
    mh,
    mh_in,
    mh_z,
    mhall,
    hft,
    hfall,
    mpt,
    mp,
    mp_in,
    owned,
    owned_in,
    left,
    right,
    lsem,
    ssem,
    rsem,
):
    NP, NH, NB = sizes
    Z, Q, NX = NP // 2, NH * NB, NH // 2
    hours, _, points = t_hbm.shape
    width = c_hbm.shape[1]
    half = width // 2
    prow = half // Q
    brow = b_hbm.shape[0]
    hh = hours // 2
    p, h, n = lax.axis_index("pts"), lax.axis_index("hrs"), lax.axis_index("bins")
    z, core = p // 2, lax.rem(p, 2)
    y_hi, x = h // NX, lax.rem(h, NX)
    q = h * NB + n
    g = 2 * core + n

    def plane(d):
        t = lax.rem(q + d, Q)
        return (p, t // NB, lax.rem(t, NB))

    def hour_block(d):
        flip = d // NX
        return (
            p,
            lax.rem(y_hi + flip, 2) * NX + lax.rem(x + d, NX),
            lax.rem(n + flip, 2),
        )

    def along_z(d):
        return (lax.rem(z + d, Z) * 2 + core, h, n)

    def quad(d):
        t = lax.rem(g + d, 4)
        return (z * 2 + t // 2, h, lax.rem(t, 2))

    other_core = (p + 1 - 2 * core, h, n)
    other_bins = (p, h, 1 - n)

    def remote(src, dst, i, target):
        return pltpu.make_async_remote_copy(
            src_ref=src,
            dst_ref=dst,
            send_sem=ssem.at[i],
            recv_sem=rsem.at[i],
            device_id=target,
            device_id_type=MESH,
        )

    def start_all(count, make, first=1):
        def body(d, _):
            make(d).start()
            return 0

        lax.fori_loop(first, count, body, 0)

    def wait_all(count, make, first=1):
        def body(d, _):
            make(d).wait()
            return 0

        lax.fori_loop(first, count, body, 0)

    def at(i, size):
        return pl.ds(pl.multiple_of(i * size, 8), size)

    base = 0

    def take(count):
        nonlocal base
        base += count
        return base - count

    my_b = at(h, brow)
    load_b = pltpu.make_async_copy(b_hbm, bbuf.at[my_b], lsem.at[hours])
    load_c = pltpu.make_async_copy(c_hbm, cbuf, lsem.at[hours + 1])
    load_b.start()
    load_c.start()

    def load_t(i):
        return pltpu.make_async_copy(t_hbm.at[i], tbuf.at[i], lsem.at[i])

    def start_t(i, _):
        load_t(i).start()
        return 0

    lax.fori_loop(0, hours, start_t, 0)

    barrier = pltpu.get_barrier_semaphore()

    def greet(make):
        def body(d, _):
            pl.semaphore_signal(
                barrier, inc=1, device_id=make(d), device_id_type=MESH
            )
            return 0

        return body

    lax.fori_loop(1, Q, greet(plane), 0)
    lax.fori_loop(1, Z, greet(along_z), 0)

    for device in (other_core, (p + 1 - 2 * core, h, 1 - n)):
        pl.semaphore_signal(barrier, inc=1, device_id=device, device_id_type=MESH)
    pl.semaphore_wait(barrier, Q - 1 + Z - 1 + 2)

    load_b.wait()
    b_base = take(NH)
    send_b = lambda d: remote(bbuf.at[my_b], bbuf.at[my_b], b_base + d, hour_block(d))
    start_all(NH, send_b)

    load_c.wait()
    chi, clo = halves(cbuf[...].T)
    ct[:width, :] = chi
    ct[width:, :] = clo

    group = 4

    def contract(i, _):
        for k in range(group):
            hour = i * group + k
            load_t(hour).wait()
            thi, tlo = halves(tbuf[hour])
            chi, clo = ct[:width, :], ct[width:, :]
            mul = functools.partial(dot, dims=((1,), (0,)))
            con[hour] = mul(chi, thi) + (mul(clo, thi) + mul(chi, tlo))
        return 0

    lax.fori_loop(0, hours // group, contract, 0)

    chi, clo = ct[:width, :], ct[width:, :]
    mul = functools.partial(dot, dims=((1,), (1,)))
    gc_part[...] = mul(chi, chi) + (mul(chi, clo) + mul(clo, chi))
    my_half = at(core, half)
    send_gc = remote(gc_part.at[my_half], gc_in, take(1), other_bins)
    send_gc.start()

    def add_up(ref, count):
        total = ref[0]
        for s in range(1, count):
            total = total + ref[s]
        return total

    wait_all(NH, send_b)
    gb_part[...] = gram(bbuf[...])
    my_rows = pl.ds(pl.multiple_of(half * core + prow * q, 8), prow)
    core_rows = pl.ds(pl.multiple_of(half * (1 - core) + prow * q, 8), prow)
    send_gb = remote(gb_part.at[core_rows], gb_in, take(1), other_core)
    send_gb.start()
    bt[...] = bbuf[...].T
    send_gb.wait()
    gb_z[z] = gb_part[my_rows, :] + gb_in[...]
    z_base = take(Z)
    send_gbz = lambda d: remote(gb_z.at[z], gb_z.at[z], z_base + d, along_z(d))
    start_all(Z, send_gbz)

    lane = lax.broadcasted_iota(jnp.int32, mht.shape, 1)

    def partial_hours(i, _):
        out = mht[...]
        for k in range(group):
            hour = i * group + k
            total = jnp.sum(con[hour] * bt[...], axis=1, keepdims=True)
            out = jnp.where(lane == hour, total, out)
        mht[...] = out
        return 0

    lax.fori_loop(0, hours // group, partial_hours, 0)
    mh[...] = mht[...].T[:hours, :]

    def tile(c2, n2):
        return at(c2, hh), pl.ds(pl.multiple_of(n2 * half, 128), half)

    my_tile = tile(core, n)
    mq_base = take(4)

    def send_mq(d):
        t = lax.rem(g + d, 4)
        return remote(
            mh.at[tile(t // 2, lax.rem(t, 2))], mh_in.at[g], mq_base + d, quad(d)
        )

    start_all(4, send_mq)
    mh_in[g] = mh[my_tile]
    mz_base = take(Z)
    send_mz = lambda d: remote(mh_z.at[z], mh_z.at[z], mz_base + d, along_z(d))
    my_hours = at(h, hours)
    ma_base = take(4)
    my_part = (
        pl.ds(pl.multiple_of(h * hours + core * hh, 8), hh),
        pl.ds(pl.multiple_of(n * half, 128), half),
    )
    send_ma = lambda d: remote(
        mhall.at[my_part], mhall.at[my_part], ma_base + d, quad(d)
    )
    mr_base = take(NH)
    send_mr = lambda d: remote(
        mhall.at[my_hours], mhall.at[my_hours], mr_base + d, hour_block(d)
    )

    wait_all(4, send_mq)
    mh_z[z] = add_up(mh_in, 4)
    start_all(Z, send_mz)

    wait_all(Z, send_gbz)
    send_gc.wait()
    gcm[my_half, :] = gc_part[my_half, :] + gc_in[...]
    swap_gc = remote(gcm.at[my_half], gcm.at[my_half], take(1), other_core)
    hmat[my_rows, :] = add_up(gb_z, Z) * gcm[my_rows, :]
    h_base = take(Q)
    send_h = lambda d: remote(hmat.at[my_rows], hmat.at[my_rows], h_base + d, plane(d))
    start_all(Q, send_h)
    swap_gc.start()

    wait_all(Z, send_mz)
    mhall[my_part] = add_up(mh_z, Z)
    start_all(4, send_ma)

    wait_all(Q, send_h)
    swap_h = remote(hmat.at[my_half], hmat.at[my_half], take(1), other_core)
    swap_h.start()
    wait_all(4, send_ma)
    start_all(NH, send_mr)
    swap_h.wait()
    invert(hmat, left, right, {})
    wait_all(NH, send_mr)
    swap_gc.wait()

    hfall[...] = jnp.dot(
        mhall[...], hmat[...], precision=HIGHEST, preferred_element_type=f32
    )
    hf = hfall[my_hours, :]
    hft[...] = hf.T
    hf_ref[...] = hf

    chunk = 32
    for rows in range(0, width, chunk):
        weights = hft[rows : rows + chunk, :]
        acc = con[0, rows : rows + chunk, :] * weights[:, 0:1]
        for i in range(1, hours):
            acc = acc + con[i, rows : rows + chunk, :] * weights[:, i : i + 1]
        mpt[rows : rows + chunk, :] = acc
    mp[...] = mpt[...].T
    mp_base = take(NH)

    def send_mp(d):
        flip = d // NX
        h2 = lax.rem(y_hi + flip, 2) * NX + lax.rem(x + d, NX)
        return remote(mp.at[at(h2, brow)], mp_in.at[d], mp_base + d, hour_block(d))

    start_all(NH, send_mp)
    hmat[...] = gram(hfall[...]) * gcm[...]
    swap_o = remote(owned, owned_in, take(1), other_bins)

    def pause_points():
        wait_all(NH, send_mp)
        total = mp[my_b, :]
        for s in range(1, NH):
            total = total + mp_in[s]
        owned[...] = total
        swap_o.start()

    invert(hmat, left, right, {13: pause_points})
    swap_o.wait()
    pf_ref[...] = jnp.dot(
        owned[...] + owned_in[...],
        hmat[...],
        precision=HIGHEST,
        preferred_element_type=f32,
    )


def local(sizes, tensor, b_factor, c_factor):
    NP, NH, NB = sizes
    Z, Q = NP // 2, NH * NB
    tensor = jnp.swapaxes(tensor, 1, 2)
    hours, bins, points = tensor.shape
    width = c_factor.shape[1]
    brow = b_factor.shape[0]
    prow = width // (2 * Q)
    hh = hours // 2
    sems = 3 * Z + Q + 3 * NH + 8 + 6
    vm = lambda *shape: pltpu.VMEM(shape, f32)
    any_spec = pl.BlockSpec(memory_space=pltpu.HBM)
    vmem_spec = pl.BlockSpec(memory_space=pltpu.VMEM)
    return pl.pallas_call(
        functools.partial(kernel, sizes),
        out_shape=(
            jax.ShapeDtypeStruct((hours, width), f32),
            jax.ShapeDtypeStruct((brow, width), f32),
        ),
        in_specs=[any_spec] * 3,
        out_specs=(vmem_spec, vmem_spec),
        scratch_shapes=[
            vm(hours, bins, points),
            vm(hours, width, points),
            vm(bins, width),
            pltpu.VMEM((2 * width, bins), bf16),
            vm(points, width),
            vm(width, points),
            vm(width, width),
            vm(prow, width),
            vm(Z, prow, width),
            vm(width, width),
            vm(width // 2, width),
            vm(width, width),
            vm(width, width),
            vm(width, 128),
            vm(hours, width),
            vm(4, hh, width // 2),
            vm(Z, hh, width // 2),
            vm(hours * NH, width),
            vm(width, hours),
            vm(hours * NH, width),
            vm(width, points),
            vm(points, width),
            vm(NH, brow, width),
            vm(brow, width),
            vm(brow, width),
            pltpu.VMEM((6 * STEP, width), bf16),
            pltpu.VMEM((6 * STEP, width), bf16),
            pltpu.SemaphoreType.DMA((hours + 2,)),
            pltpu.SemaphoreType.DMA((sems,)),
            pltpu.SemaphoreType.DMA((sems,)),
        ],
        compiler_params=pltpu.CompilerParams(
            collective_id=0,
            has_side_effects=True,
            vmem_limit_bytes=56 * 1024 * 1024,
        ),
    )(tensor, b_factor, c_factor)


def solution(mesh):
    sizes = (mesh.shape["pts"], mesh.shape["hrs"], mesh.shape["bins"])
    placed = (P("hrs", "pts", "bins"), P(("pts", "hrs"), None), P("bins", None))
    return jax.shard_map(
        functools.partial(local, sizes),
        mesh=mesh,
        in_specs=placed,
        out_specs=(P("hrs", None), P(("pts", "hrs"), None)),
        check_vma=False,
    )
```

```python
import functools

import jax
import jax.numpy as jnp
from jax import lax
from jax.experimental import pallas as pl
from jax.experimental.pallas import tpu as pltpu
from jax.sharding import PartitionSpec as P

f32 = jnp.float32
bf16 = jnp.bfloat16
HIGHEST = lax.Precision.HIGHEST
MESH = pl.DeviceIdType.MESH
CONTRACT_ROWS = (((0,), (0,)), ((), ()))


def dot(a, b, dims):
    return lax.dot_general(a, b, (dims, ((), ())), preferred_element_type=f32)


def halves(x):
    hi = x.astype(bf16)
    return hi, (x - hi.astype(f32)).astype(bf16)


def gram(x):
    hi = x.astype(bf16).astype(f32)
    lo = x - hi
    left = jnp.concatenate([hi, hi, lo], axis=0).astype(bf16)
    right = jnp.concatenate([hi, lo, hi], axis=0).astype(bf16)
    return dot(left, right, ((0,), (0,)))


def split(x):
    first = x.astype(bf16).astype(f32)
    rest = x - first
    second = rest.astype(bf16).astype(f32)
    return first, second, rest - second


STEP = 16


def spread_lanes(x, first):
    return [
        jnp.take_along_axis(
            x,
            jnp.full(x.shape, first + j, jnp.int32),
            axis=1,
            mode="promise_in_bounds",
        )
        for j in range(STEP)
    ]


def spread_row(x, j):
    return jnp.broadcast_to(x[j : j + 1, :], x.shape)


def lane_tile(x, t):
    return jnp.where(t == 0, x[:, :128], x[:, 128:])


def pivot(panel, row):
    lane = lax.broadcasted_iota(jnp.int32, panel.shape, 1)
    sub = lax.broadcasted_iota(jnp.int32, panel.shape, 0)
    rel = lane - row
    t = row // 128
    cols = spread_lanes(lane_tile(panel, t), row - t * 128)
    work = jnp.where((rel >= 0) & (rel < STEP), jnp.where(rel == sub, 1.0, 0.0), panel)
    data = [work[:, :128], work[:, 128:]]
    sub = lax.broadcasted_iota(jnp.int32, (STEP, 128), 0)
    for j in range(STEP):
        state = cols[j:] + data
        rows = [spread_row(x, j) for x in state]
        inverse = pltpu.reciprocal(rows[0], approx=False)
        factor = jnp.where(sub == j, 1.0 - inverse, cols[j] * inverse)
        state = [x - factor * r for x, r in zip(state, rows)]
        cols = cols[:j] + state[: STEP - j]
        data = state[STEP - j :]
    column = jnp.where(lane < row, -panel, panel)
    return jnp.concatenate(data, axis=1), column


def follow(rows, done, row):
    rel = lax.broadcasted_iota(jnp.int32, rows.shape, 1) - row
    t = row // 128
    cols = spread_lanes(lane_tile(rows, t), row - t * 128)
    rows = jnp.where((rel >= 0) & (rel < STEP), 0.0, rows)
    out = []
    for s in (0, 128):
        part = done[:, s : s + 128]
        terms = [cols[j] * spread_row(part, j) for j in range(STEP)]
        while len(terms) > 1:
            terms = [x + y for x, y in zip(terms[::2], terms[1::2])]
        out.append(rows[:, s : s + 128] - terms[0])
    return jnp.concatenate(out, axis=1)


def factors(left, right, column, done):
    c1, c2, c3 = split(column)
    r1, r2, r3 = split(done)
    left[...] = jnp.concatenate([c1, c1, c2, c2, c1, c3], axis=0).astype(bf16)
    right[...] = jnp.concatenate([r1, r2, r1, r2, r3, r1], axis=0).astype(bf16)


def late_update(a, left, right, row, done):
    update = lax.dot_general(
        left[...], right[...], CONTRACT_ROWS, preferred_element_type=f32
    )
    rel = lax.broadcasted_iota(jnp.int32, a.shape, 1) - row
    a[...] = jnp.where((rel >= 0) & (rel < STEP), 0.0, a[...]) - update
    a[pl.ds(row, STEP), :] = done


def invert(a, left, right, pauses):
    steps = a.shape[0] // STEP

    def at(k):
        return pl.multiple_of(k * STEP, STEP)

    done, column = pivot(a[0:STEP, :], 0)
    factors(left, right, column, done)
    panel = follow(a[STEP : 2 * STEP, :], done, 0)

    def body(k, carry):
        panel, before = carry
        late_update(a, left, right, at(k - 1), before)
        done, column = pivot(panel, at(k))
        panel = follow(a[pl.ds(at(k + 1), STEP), :], done, at(k))
        factors(left, right, column, done)
        return panel, done

    carry = (panel, done)
    first = 1
    for stop in sorted(pauses):
        carry = lax.fori_loop(first, stop, body, carry)
        pauses[stop]()
        first = stop
    panel, before = lax.fori_loop(first, steps - 1, body, carry)
    late_update(a, left, right, at(steps - 2), before)
    done, column = pivot(panel, at(steps - 1))
    factors(left, right, column, done)
    late_update(a, left, right, at(steps - 1), done)


def kernel(
    sizes,
    t_hbm,
    b_hbm,
    c_hbm,
    hf_ref,
    pf_ref,
    tbuf,
    con,
    cbuf,
    ct,
    bbuf,
    bt,
    gb_part,
    gb_in,
    gb_z,
    gc_part,
    gc_in,
    hmat,
    gcm,
    mht,
    mh,
    mh_in,
    mh_z,
    mhall,
    hft,
    hfall,
    mpt,
    mp,
    mp_in,
    owned,
    owned_in,
    left,
    right,
    lsem,
    ssem,
    rsem,
):
    NP, NH, NB = sizes
    Z, Q, NX = NP // 2, NH * NB, NH // 2
    hours, _, points = t_hbm.shape
    width = c_hbm.shape[1]
    half = width // 2
    prow = half // Q
    brow = b_hbm.shape[0]
    hh = hours // 2
    p, h, n = lax.axis_index("pts"), lax.axis_index("hrs"), lax.axis_index("bins")
    z, core = p // 2, lax.rem(p, 2)
    y_hi, x = h // NX, lax.rem(h, NX)
    q = h * NB + n
    g = 2 * core + n

    def plane(d):
        t = lax.rem(q + d, Q)
        return (p, t // NB, lax.rem(t, NB))

    def hour_block(d):
        flip = d // NX
        return (
            p,
            lax.rem(y_hi + flip, 2) * NX + lax.rem(x + d, NX),
            lax.rem(n + flip, 2),
        )

    def along_z(d):
        return (lax.rem(z + d, Z) * 2 + core, h, n)

    def quad(d):
        t = lax.rem(g + d, 4)
        return (z * 2 + t // 2, h, lax.rem(t, 2))

    other_core = (p + 1 - 2 * core, h, n)
    other_bins = (p, h, 1 - n)

    def remote(src, dst, i, target):
        return pltpu.make_async_remote_copy(
            src_ref=src,
            dst_ref=dst,
            send_sem=ssem.at[i],
            recv_sem=rsem.at[i],
            device_id=target,
            device_id_type=MESH,
        )

    def start_all(count, make, first=1):
        def body(d, _):
            make(d).start()
            return 0

        lax.fori_loop(first, count, body, 0)

    def wait_all(count, make, first=1):
        def body(d, _):
            make(d).wait()
            return 0

        lax.fori_loop(first, count, body, 0)

    def at(i, size):
        return pl.ds(pl.multiple_of(i * size, 8), size)

    base = 0

    def take(count):
        nonlocal base
        base += count
        return base - count

    my_b = at(h, brow)
    load_b = pltpu.make_async_copy(b_hbm, bbuf.at[my_b], lsem.at[hours])
    load_c = pltpu.make_async_copy(c_hbm, cbuf, lsem.at[hours + 1])
    load_b.start()
    load_c.start()

    def load_t(i):
        return pltpu.make_async_copy(t_hbm.at[i], tbuf.at[i], lsem.at[i])

    def start_t(i, _):
        load_t(i).start()
        return 0

    lax.fori_loop(0, hours, start_t, 0)

    barrier = pltpu.get_barrier_semaphore()

    def greet(make):
        def body(d, _):
            pl.semaphore_signal(
                barrier, inc=1, device_id=make(d), device_id_type=MESH
            )
            return 0

        return body

    lax.fori_loop(1, Q, greet(plane), 0)
    lax.fori_loop(1, Z, greet(along_z), 0)

    for device in (other_core, (p + 1 - 2 * core, h, 1 - n)):
        pl.semaphore_signal(barrier, inc=1, device_id=device, device_id_type=MESH)
    pl.semaphore_wait(barrier, Q - 1 + Z - 1 + 2)

    load_b.wait()
    b_base = take(NH)
    send_b = lambda d: remote(bbuf.at[my_b], bbuf.at[my_b], b_base + d, hour_block(d))
    start_all(NH, send_b)

    load_c.wait()
    chi, clo = halves(cbuf[...].T)
    ct[:width, :] = chi
    ct[width:, :] = clo

    group = 4

    def contract(i, _):
        for k in range(group):
            load_t(i * group + k).wait()
        for k in range(group):
            hour = i * group + k
            thi, tlo = halves(tbuf[hour])
            chi, clo = ct[:width, :], ct[width:, :]
            mul = functools.partial(dot, dims=((1,), (0,)))
            con[hour] = mul(chi, thi) + (mul(clo, thi) + mul(chi, tlo))
        return 0

    lax.fori_loop(0, hours // group, contract, 0)

    chi, clo = ct[:width, :], ct[width:, :]
    mul = functools.partial(dot, dims=((1,), (1,)))
    gc_part[...] = mul(chi, chi) + (mul(chi, clo) + mul(clo, chi))
    my_half = at(core, half)
    send_gc = remote(gc_part.at[my_half], gc_in, take(1), other_bins)
    send_gc.start()

    def add_up(ref, count):
        total = ref[0]
        for s in range(1, count):
            total = total + ref[s]
        return total

    wait_all(NH, send_b)
    gb_part[...] = gram(bbuf[...])
    my_rows = pl.ds(pl.multiple_of(half * core + prow * q, 8), prow)
    core_rows = pl.ds(pl.multiple_of(half * (1 - core) + prow * q, 8), prow)
    send_gb = remote(gb_part.at[core_rows], gb_in, take(1), other_core)
    send_gb.start()
    bt[...] = bbuf[...].T
    send_gb.wait()
    gb_z[z] = gb_part[my_rows, :] + gb_in[...]
    z_base = take(Z)
    send_gbz = lambda d: remote(gb_z.at[z], gb_z.at[z], z_base + d, along_z(d))
    start_all(Z, send_gbz)

    lane = lax.broadcasted_iota(jnp.int32, mht.shape, 1)

    def partial_hours(i, _):
        out = mht[...]
        for k in range(group):
            hour = i * group + k
            total = jnp.sum(con[hour] * bt[...], axis=1, keepdims=True)
            out = jnp.where(lane == hour, total, out)
        mht[...] = out
        return 0

    lax.fori_loop(0, hours // group, partial_hours, 0)
    mh[...] = mht[...].T[:hours, :]

    def tile(c2, n2):
        return at(c2, hh), pl.ds(pl.multiple_of(n2 * half, 128), half)

    my_tile = tile(core, n)
    mq_base = take(4)

    def send_mq(d):
        t = lax.rem(g + d, 4)
        return remote(
            mh.at[tile(t // 2, lax.rem(t, 2))], mh_in.at[g], mq_base + d, quad(d)
        )

    start_all(4, send_mq)
    mh_in[g] = mh[my_tile]
    mz_base = take(Z)
    send_mz = lambda d: remote(mh_z.at[z], mh_z.at[z], mz_base + d, along_z(d))
    my_hours = at(h, hours)
    ma_base = take(4)
    my_part = (
        pl.ds(pl.multiple_of(h * hours + core * hh, 8), hh),
        pl.ds(pl.multiple_of(n * half, 128), half),
    )
    send_ma = lambda d: remote(
        mhall.at[my_part], mhall.at[my_part], ma_base + d, quad(d)
    )
    mr_base = take(NH)
    send_mr = lambda d: remote(
        mhall.at[my_hours], mhall.at[my_hours], mr_base + d, hour_block(d)
    )

    wait_all(4, send_mq)
    mh_z[z] = add_up(mh_in, 4)
    start_all(Z, send_mz)

    wait_all(Z, send_gbz)
    send_gc.wait()
    gcm[my_half, :] = gc_part[my_half, :] + gc_in[...]
    swap_gc = remote(gcm.at[my_half], gcm.at[my_half], take(1), other_core)
    hmat[my_rows, :] = add_up(gb_z, Z) * gcm[my_rows, :]
    h_base = take(Q)
    send_h = lambda d: remote(hmat.at[my_rows], hmat.at[my_rows], h_base + d, plane(d))
    start_all(Q, send_h)
    swap_gc.start()

    wait_all(Z, send_mz)
    mhall[my_part] = add_up(mh_z, Z)
    start_all(4, send_ma)

    wait_all(Q, send_h)
    swap_h = remote(hmat.at[my_half], hmat.at[my_half], take(1), other_core)
    swap_h.start()
    wait_all(4, send_ma)
    start_all(NH, send_mr)
    swap_h.wait()
    invert(hmat, left, right, {})
    wait_all(NH, send_mr)
    swap_gc.wait()

    hfall[...] = jnp.dot(
        mhall[...], hmat[...], precision=HIGHEST, preferred_element_type=f32
    )
    hf = hfall[my_hours, :]
    hft[...] = hf.T
    hf_ref[...] = hf

    chunk = 32
    for rows in range(0, width, chunk):
        weights = hft[rows : rows + chunk, :]
        acc = con[0, rows : rows + chunk, :] * weights[:, 0:1]
        for i in range(1, hours):
            acc = acc + con[i, rows : rows + chunk, :] * weights[:, i : i + 1]
        mpt[rows : rows + chunk, :] = acc
    mp[...] = mpt[...].T
    mp_base = take(NH)

    def send_mp(d):
        flip = d // NX
        h2 = lax.rem(y_hi + flip, 2) * NX + lax.rem(x + d, NX)
        return remote(mp.at[at(h2, brow)], mp_in.at[d], mp_base + d, hour_block(d))

    start_all(NH, send_mp)
    hmat[...] = gram(hfall[...]) * gcm[...]
    swap_o = remote(owned, owned_in, take(1), other_bins)

    def pause_points():
        wait_all(NH, send_mp)
        total = mp[my_b, :]
        for s in range(1, NH):
            total = total + mp_in[s]
        owned[...] = total
        swap_o.start()

    invert(hmat, left, right, {13: pause_points})
    swap_o.wait()
    pf_ref[...] = jnp.dot(
        owned[...] + owned_in[...],
        hmat[...],
        precision=HIGHEST,
        preferred_element_type=f32,
    )


def write_out(hf_in, pf_in, hf_out, pf_out, sem):
    copies = [
        pltpu.make_async_copy(hf_in, hf_out, sem.at[0]),
        pltpu.make_async_copy(pf_in, pf_out, sem.at[1]),
    ]
    for copy in copies:
        copy.start()
    for copy in copies:
        copy.wait()


def local(sizes, tensor, b_factor, c_factor):
    NP, NH, NB = sizes
    Z, Q = NP // 2, NH * NB
    tensor = jnp.swapaxes(tensor, 1, 2)
    hours, bins, points = tensor.shape
    width = c_factor.shape[1]
    brow = b_factor.shape[0]
    prow = width // (2 * Q)
    hh = hours // 2
    sems = 3 * Z + Q + 3 * NH + 8 + 6
    vm = lambda *shape: pltpu.VMEM(shape, f32)
    any_spec = pl.BlockSpec(memory_space=pltpu.HBM)
    vmem_spec = pl.BlockSpec(memory_space=pltpu.VMEM)
    out_shape = (
        jax.ShapeDtypeStruct((hours, width), f32),
        jax.ShapeDtypeStruct((brow, width), f32),
    )
    results = pl.pallas_call(
        functools.partial(kernel, sizes),
        out_shape=out_shape,
        in_specs=[any_spec] * 3,
        out_specs=(vmem_spec, vmem_spec),
        scratch_shapes=[
            vm(hours, bins, points),
            vm(hours, width, points),
            vm(bins, width),
            pltpu.VMEM((2 * width, bins), bf16),
            vm(points, width),
            vm(width, points),
            vm(width, width),
            vm(prow, width),
            vm(Z, prow, width),
            vm(width, width),
            vm(width // 2, width),
            vm(width, width),
            vm(width, width),
            vm(width, 128),
            vm(hours, width),
            vm(4, hh, width // 2),
            vm(Z, hh, width // 2),
            vm(hours * NH, width),
            vm(width, hours),
            vm(hours * NH, width),
            vm(width, points),
            vm(points, width),
            vm(NH, brow, width),
            vm(brow, width),
            vm(brow, width),
            pltpu.VMEM((6 * STEP, width), bf16),
            pltpu.VMEM((6 * STEP, width), bf16),
            pltpu.SemaphoreType.DMA((hours + 2,)),
            pltpu.SemaphoreType.DMA((sems,)),
            pltpu.SemaphoreType.DMA((sems,)),
        ],
        compiler_params=pltpu.CompilerParams(
            collective_id=0,
            has_side_effects=True,
            vmem_limit_bytes=56 * 1024 * 1024,
        ),
    )(tensor, b_factor, c_factor)
    outer = pl.BlockSpec(memory_space=pl.ANY)
    return pl.pallas_call(
        write_out,
        out_shape=out_shape,
        in_specs=[outer] * 2,
        out_specs=(outer, outer),
        scratch_shapes=[pltpu.SemaphoreType.DMA((2,))],
    )(*results)


def solution(mesh):
    sizes = (mesh.shape["pts"], mesh.shape["hrs"], mesh.shape["bins"])
    placed = (P("hrs", "pts", "bins"), P(("pts", "hrs"), None), P("bins", None))
    return jax.shard_map(
        functools.partial(local, sizes),
        mesh=mesh,
        in_specs=placed,
        out_specs=(P("hrs", None), P(("pts", "hrs"), None)),
        check_vma=False,
    )
```

```python
import functools

import jax
import jax.numpy as jnp
from jax import lax
from jax.experimental import pallas as pl
from jax.experimental.pallas import tpu as pltpu
from jax.sharding import PartitionSpec as P

f32 = jnp.float32
bf16 = jnp.bfloat16
HIGHEST = lax.Precision.HIGHEST
MESH = pl.DeviceIdType.MESH
CONTRACT_ROWS = (((0,), (0,)), ((), ()))


def dot(a, b, dims):
    return lax.dot_general(a, b, (dims, ((), ())), preferred_element_type=f32)


def halves(x):
    hi = x.astype(bf16)
    return hi, (x - hi.astype(f32)).astype(bf16)


def gram(x):
    hi = x.astype(bf16).astype(f32)
    lo = x - hi
    left = jnp.concatenate([hi, hi, lo], axis=0).astype(bf16)
    right = jnp.concatenate([hi, lo, hi], axis=0).astype(bf16)
    return dot(left, right, ((0,), (0,)))


def split(x):
    first = x.astype(bf16).astype(f32)
    rest = x - first
    second = rest.astype(bf16).astype(f32)
    return first, second, rest - second


STEP = 16


def spread_lanes(x, first):
    return [
        jnp.take_along_axis(
            x,
            jnp.full(x.shape, first + j, jnp.int32),
            axis=1,
            mode="promise_in_bounds",
        )
        for j in range(STEP)
    ]


def spread_row(x, j):
    return jnp.broadcast_to(x[j : j + 1, :], x.shape)


def lane_tile(x, t):
    return jnp.where(t == 0, x[:, :128], x[:, 128:])


def pivot(panel, row):
    lane = lax.broadcasted_iota(jnp.int32, panel.shape, 1)
    sub = lax.broadcasted_iota(jnp.int32, panel.shape, 0)
    rel = lane - row
    t = row // 128
    cols = spread_lanes(lane_tile(panel, t), row - t * 128)
    work = jnp.where((rel >= 0) & (rel < STEP), jnp.where(rel == sub, 1.0, 0.0), panel)
    data = [work[:, :128], work[:, 128:]]
    sub = lax.broadcasted_iota(jnp.int32, (STEP, 128), 0)
    for j in range(STEP):
        state = cols[j:] + data
        rows = [spread_row(x, j) for x in state]
        inverse = pltpu.reciprocal(rows[0], approx=False)
        factor = jnp.where(sub == j, 1.0 - inverse, cols[j] * inverse)
        state = [x - factor * r for x, r in zip(state, rows)]
        cols = cols[:j] + state[: STEP - j]
        data = state[STEP - j :]
    column = jnp.where(lane < row, -panel, panel)
    return jnp.concatenate(data, axis=1), column


def follow(rows, done, row):
    rel = lax.broadcasted_iota(jnp.int32, rows.shape, 1) - row
    t = row // 128
    cols = spread_lanes(lane_tile(rows, t), row - t * 128)
    rows = jnp.where((rel >= 0) & (rel < STEP), 0.0, rows)
    out = []
    for s in (0, 128):
        part = done[:, s : s + 128]
        terms = [cols[j] * spread_row(part, j) for j in range(STEP)]
        while len(terms) > 1:
            terms = [x + y for x, y in zip(terms[::2], terms[1::2])]
        out.append(rows[:, s : s + 128] - terms[0])
    return jnp.concatenate(out, axis=1)


def factors(left, right, column, done):
    c1, c2, c3 = split(column)
    r1, r2, r3 = split(done)
    left[...] = jnp.concatenate([c1, c1, c2, c2, c1, c3], axis=0).astype(bf16)
    right[...] = jnp.concatenate([r1, r2, r1, r2, r3, r1], axis=0).astype(bf16)


def late_update(a, left, right, row, done):
    update = lax.dot_general(
        left[...], right[...], CONTRACT_ROWS, preferred_element_type=f32
    )
    rel = lax.broadcasted_iota(jnp.int32, a.shape, 1) - row
    a[...] = jnp.where((rel >= 0) & (rel < STEP), 0.0, a[...]) - update
    a[pl.ds(row, STEP), :] = done


def invert(a, left, right, pauses):
    steps = a.shape[0] // STEP

    def at(k):
        return pl.multiple_of(k * STEP, STEP)

    done, column = pivot(a[0:STEP, :], 0)
    factors(left, right, column, done)
    panel = follow(a[STEP : 2 * STEP, :], done, 0)

    def body(k, carry):
        panel, before = carry
        late_update(a, left, right, at(k - 1), before)
        done, column = pivot(panel, at(k))
        panel = follow(a[pl.ds(at(k + 1), STEP), :], done, at(k))
        factors(left, right, column, done)
        return panel, done

    carry = (panel, done)
    first = 1
    for stop in sorted(pauses):
        carry = lax.fori_loop(first, stop, body, carry, unroll=2)
        pauses[stop]()
        first = stop
    panel, before = lax.fori_loop(first, steps - 1, body, carry, unroll=2)
    late_update(a, left, right, at(steps - 2), before)
    done, column = pivot(panel, at(steps - 1))
    factors(left, right, column, done)
    late_update(a, left, right, at(steps - 1), done)


def kernel(
    sizes,
    t_hbm,
    b_hbm,
    c_hbm,
    hf_ref,
    pf_ref,
    tbuf,
    con,
    cbuf,
    ct,
    bbuf,
    bt,
    gb_part,
    gb_in,
    gb_z,
    gc_part,
    gc_in,
    hmat,
    gcm,
    mht,
    mh,
    mh_in,
    mh_z,
    mhall,
    hft,
    hfall,
    mpt,
    mp,
    mp_in,
    owned,
    owned_in,
    left,
    right,
    lsem,
    ssem,
    rsem,
):
    NP, NH, NB = sizes
    Z, Q, NX = NP // 2, NH * NB, NH // 2
    hours, _, points = t_hbm.shape
    width = c_hbm.shape[1]
    half = width // 2
    prow = half // Q
    brow = b_hbm.shape[0]
    hh = hours // 2
    p, h, n = lax.axis_index("pts"), lax.axis_index("hrs"), lax.axis_index("bins")
    z, core = p // 2, lax.rem(p, 2)
    y_hi, x = h // NX, lax.rem(h, NX)
    q = h * NB + n
    g = 2 * core + n

    def plane(d):
        t = lax.rem(q + d, Q)
        return (p, t // NB, lax.rem(t, NB))

    def hour_block(d):
        flip = d // NX
        return (
            p,
            lax.rem(y_hi + flip, 2) * NX + lax.rem(x + d, NX),
            lax.rem(n + flip, 2),
        )

    def along_z(d):
        return (lax.rem(z + d, Z) * 2 + core, h, n)

    def quad(d):
        t = lax.rem(g + d, 4)
        return (z * 2 + t // 2, h, lax.rem(t, 2))

    other_core = (p + 1 - 2 * core, h, n)
    other_bins = (p, h, 1 - n)

    def remote(src, dst, i, target):
        return pltpu.make_async_remote_copy(
            src_ref=src,
            dst_ref=dst,
            send_sem=ssem.at[i],
            recv_sem=rsem.at[i],
            device_id=target,
            device_id_type=MESH,
        )

    def start_all(count, make, first=1):
        def body(d, _):
            make(d).start()
            return 0

        lax.fori_loop(first, count, body, 0)

    def wait_all(count, make, first=1):
        def body(d, _):
            make(d).wait()
            return 0

        lax.fori_loop(first, count, body, 0)

    def at(i, size):
        return pl.ds(pl.multiple_of(i * size, 8), size)

    base = 0

    def take(count):
        nonlocal base
        base += count
        return base - count

    my_b = at(h, brow)
    load_b = pltpu.make_async_copy(b_hbm, bbuf.at[my_b], lsem.at[hours])
    load_c = pltpu.make_async_copy(c_hbm, cbuf, lsem.at[hours + 1])
    load_b.start()
    load_c.start()

    def load_t(i):
        return pltpu.make_async_copy(t_hbm.at[i], tbuf.at[i], lsem.at[i])

    def start_t(i, _):
        load_t(i).start()
        return 0

    lax.fori_loop(0, hours, start_t, 0)

    barrier = pltpu.get_barrier_semaphore()

    def greet(make):
        def body(d, _):
            pl.semaphore_signal(
                barrier, inc=1, device_id=make(d), device_id_type=MESH
            )
            return 0

        return body

    lax.fori_loop(1, Q, greet(plane), 0)
    lax.fori_loop(1, Z, greet(along_z), 0)

    for device in (other_core, (p + 1 - 2 * core, h, 1 - n)):
        pl.semaphore_signal(barrier, inc=1, device_id=device, device_id_type=MESH)
    pl.semaphore_wait(barrier, Q - 1 + Z - 1 + 2)

    load_b.wait()
    b_base = take(NH)
    send_b = lambda d: remote(bbuf.at[my_b], bbuf.at[my_b], b_base + d, hour_block(d))
    start_all(NH, send_b)

    load_c.wait()
    chi, clo = halves(cbuf[...].T)
    ct[:width, :] = chi
    ct[width:, :] = clo

    group = 4

    def contract(i, _):
        for k in range(group):
            load_t(i * group + k).wait()
        for k in range(group):
            hour = i * group + k
            thi, tlo = halves(tbuf[hour])
            chi, clo = ct[:width, :], ct[width:, :]
            mul = functools.partial(dot, dims=((1,), (0,)))
            con[hour] = mul(chi, thi) + (mul(clo, thi) + mul(chi, tlo))
        return 0

    lax.fori_loop(0, hours // group, contract, 0)

    chi, clo = ct[:width, :], ct[width:, :]
    mul = functools.partial(dot, dims=((1,), (1,)))
    gc_part[...] = mul(chi, chi) + (mul(chi, clo) + mul(clo, chi))
    my_half = at(core, half)
    send_gc = remote(gc_part.at[my_half], gc_in, take(1), other_bins)
    send_gc.start()

    def add_up(ref, count):
        total = ref[0]
        for s in range(1, count):
            total = total + ref[s]
        return total

    wait_all(NH, send_b)
    gb_part[...] = gram(bbuf[...])
    my_rows = pl.ds(pl.multiple_of(half * core + prow * q, 8), prow)
    core_rows = pl.ds(pl.multiple_of(half * (1 - core) + prow * q, 8), prow)
    send_gb = remote(gb_part.at[core_rows], gb_in, take(1), other_core)
    send_gb.start()
    bt[...] = bbuf[...].T
    send_gb.wait()
    gb_z[z] = gb_part[my_rows, :] + gb_in[...]
    z_base = take(Z)
    send_gbz = lambda d: remote(gb_z.at[z], gb_z.at[z], z_base + d, along_z(d))
    start_all(Z, send_gbz)

    lane = lax.broadcasted_iota(jnp.int32, mht.shape, 1)

    def partial_hours(i, _):
        out = mht[...]
        for k in range(group):
            hour = i * group + k
            total = jnp.sum(con[hour] * bt[...], axis=1, keepdims=True)
            out = jnp.where(lane == hour, total, out)
        mht[...] = out
        return 0

    lax.fori_loop(0, hours // group, partial_hours, 0)
    mh[...] = mht[...].T[:hours, :]

    def tile(c2, n2):
        return at(c2, hh), pl.ds(pl.multiple_of(n2 * half, 128), half)

    my_tile = tile(core, n)
    mq_base = take(4)

    def send_mq(d):
        t = lax.rem(g + d, 4)
        return remote(
            mh.at[tile(t // 2, lax.rem(t, 2))], mh_in.at[g], mq_base + d, quad(d)
        )

    start_all(4, send_mq)
    mh_in[g] = mh[my_tile]
    mz_base = take(Z)
    send_mz = lambda d: remote(mh_z.at[z], mh_z.at[z], mz_base + d, along_z(d))
    my_hours = at(h, hours)
    ma_base = take(4)
    my_part = (
        pl.ds(pl.multiple_of(h * hours + core * hh, 8), hh),
        pl.ds(pl.multiple_of(n * half, 128), half),
    )
    send_ma = lambda d: remote(
        mhall.at[my_part], mhall.at[my_part], ma_base + d, quad(d)
    )
    mr_base = take(NH)
    send_mr = lambda d: remote(
        mhall.at[my_hours], mhall.at[my_hours], mr_base + d, hour_block(d)
    )

    wait_all(4, send_mq)
    mh_z[z] = add_up(mh_in, 4)
    start_all(Z, send_mz)

    wait_all(Z, send_gbz)
    send_gc.wait()
    gcm[my_half, :] = gc_part[my_half, :] + gc_in[...]
    swap_gc = remote(gcm.at[my_half], gcm.at[my_half], take(1), other_core)
    hmat[my_rows, :] = add_up(gb_z, Z) * gcm[my_rows, :]
    h_base = take(Q)
    send_h = lambda d: remote(hmat.at[my_rows], hmat.at[my_rows], h_base + d, plane(d))
    start_all(Q, send_h)
    swap_gc.start()

    wait_all(Z, send_mz)
    mhall[my_part] = add_up(mh_z, Z)
    start_all(4, send_ma)

    wait_all(Q, send_h)
    swap_h = remote(hmat.at[my_half], hmat.at[my_half], take(1), other_core)
    swap_h.start()
    wait_all(4, send_ma)
    start_all(NH, send_mr)
    swap_h.wait()
    invert(hmat, left, right, {})

    hour_rows = functools.partial(
        jnp.dot, precision=HIGHEST, preferred_element_type=f32
    )
    hf = hour_rows(mhall[my_hours, :], hmat[...])
    hft[...] = hf.T
    hf_ref[...] = hf

    chunk = 32
    for rows in range(0, width, chunk):
        weights = hft[rows : rows + chunk, :]
        acc = con[0, rows : rows + chunk, :] * weights[:, 0:1]
        for i in range(1, hours):
            acc = acc + con[i, rows : rows + chunk, :] * weights[:, i : i + 1]
        mpt[rows : rows + chunk, :] = acc
    mp[...] = mpt[...].T
    mp_base = take(NH)

    def send_mp(d):
        flip = d // NX
        h2 = lax.rem(y_hi + flip, 2) * NX + lax.rem(x + d, NX)
        return remote(mp.at[at(h2, brow)], mp_in.at[d], mp_base + d, hour_block(d))

    start_all(NH, send_mp)

    wait_all(NH, send_mr)
    swap_gc.wait()
    hfall[...] = hour_rows(mhall[...], hmat[...])
    hmat[...] = gram(hfall[...]) * gcm[...]
    swap_o = remote(owned, owned_in, take(1), other_bins)

    def pause_points():
        wait_all(NH, send_mp)
        total = mp[my_b, :]
        for s in range(1, NH):
            total = total + mp_in[s]
        owned[...] = total
        swap_o.start()

    invert(hmat, left, right, {13: pause_points})
    swap_o.wait()
    pf_ref[...] = jnp.dot(
        owned[...] + owned_in[...],
        hmat[...],
        precision=HIGHEST,
        preferred_element_type=f32,
    )


def local(sizes, tensor, b_factor, c_factor):
    NP, NH, NB = sizes
    Z, Q = NP // 2, NH * NB
    tensor = jnp.swapaxes(tensor, 1, 2)
    hours, bins, points = tensor.shape
    width = c_factor.shape[1]
    brow = b_factor.shape[0]
    prow = width // (2 * Q)
    hh = hours // 2
    sems = 3 * Z + Q + 3 * NH + 8 + 6
    vm = lambda *shape: pltpu.VMEM(shape, f32)
    any_spec = pl.BlockSpec(memory_space=pltpu.HBM)
    vmem_spec = pl.BlockSpec(memory_space=pltpu.VMEM)
    out_shape = (
        jax.ShapeDtypeStruct((hours, width), f32),
        jax.ShapeDtypeStruct((brow, width), f32),
    )
    return pl.pallas_call(
        functools.partial(kernel, sizes),
        out_shape=out_shape,
        in_specs=[any_spec] * 3,
        out_specs=(vmem_spec, vmem_spec),
        scratch_shapes=[
            vm(hours, bins, points),
            vm(hours, width, points),
            vm(bins, width),
            pltpu.VMEM((2 * width, bins), bf16),
            vm(points, width),
            vm(width, points),
            vm(width, width),
            vm(prow, width),
            vm(Z, prow, width),
            vm(width, width),
            vm(width // 2, width),
            vm(width, width),
            vm(width, width),
            vm(width, 128),
            vm(hours, width),
            vm(4, hh, width // 2),
            vm(Z, hh, width // 2),
            vm(hours * NH, width),
            vm(width, hours),
            vm(hours * NH, width),
            vm(width, points),
            vm(points, width),
            vm(NH, brow, width),
            vm(brow, width),
            vm(brow, width),
            pltpu.VMEM((6 * STEP, width), bf16),
            pltpu.VMEM((6 * STEP, width), bf16),
            pltpu.SemaphoreType.DMA((hours + 2,)),
            pltpu.SemaphoreType.DMA((sems,)),
            pltpu.SemaphoreType.DMA((sems,)),
        ],
        compiler_params=pltpu.CompilerParams(
            collective_id=0,
            has_side_effects=True,
            vmem_limit_bytes=54784 * 1024,
        ),
    )(tensor, b_factor, c_factor)


def solution(mesh):
    sizes = (mesh.shape["pts"], mesh.shape["hrs"], mesh.shape["bins"])
    placed = (P("hrs", "pts", "bins"), P(("pts", "hrs"), None), P("bins", None))
    return jax.shard_map(
        functools.partial(local, sizes),
        mesh=mesh,
        in_specs=placed,
        out_specs=(P("hrs", None), P(("pts", "hrs"), None)),
        check_vma=False,
    )
```

```python
import functools

import jax
import jax.numpy as jnp
from jax import lax
from jax.experimental import pallas as pl
from jax.experimental.pallas import tpu as pltpu
from jax.sharding import PartitionSpec as P

f32 = jnp.float32
bf16 = jnp.bfloat16
HIGHEST = lax.Precision.HIGHEST
MESH = pl.DeviceIdType.MESH
CONTRACT_ROWS = (((0,), (0,)), ((), ()))


def dot(a, b, dims):
    return lax.dot_general(a, b, (dims, ((), ())), preferred_element_type=f32)


def halves(x):
    hi = x.astype(bf16)
    return hi, (x - hi.astype(f32)).astype(bf16)


def gram(x):
    hi = x.astype(bf16).astype(f32)
    lo = x - hi
    left = jnp.concatenate([hi, hi, lo], axis=0).astype(bf16)
    right = jnp.concatenate([hi, lo, hi], axis=0).astype(bf16)
    return dot(left, right, ((0,), (0,)))


def split(x):
    first = x.astype(bf16).astype(f32)
    rest = x - first
    second = rest.astype(bf16).astype(f32)
    return first, second, rest - second


STEP = 16


def spread_lanes(x, first):
    return [
        jnp.take_along_axis(
            x,
            jnp.full(x.shape, first + j, jnp.int32),
            axis=1,
            mode="promise_in_bounds",
        )
        for j in range(STEP)
    ]


def spread_row(x, j):
    return jnp.broadcast_to(x[j : j + 1, :], x.shape)


def lane_tile(x, t):
    return jnp.where(t == 0, x[:, :128], x[:, 128:])


def pivot(panel, row):
    lane = lax.broadcasted_iota(jnp.int32, panel.shape, 1)
    sub = lax.broadcasted_iota(jnp.int32, panel.shape, 0)
    rel = lane - row
    t = row // 128
    cols = spread_lanes(lane_tile(panel, t), row - t * 128)
    work = jnp.where((rel >= 0) & (rel < STEP), jnp.where(rel == sub, 1.0, 0.0), panel)
    data = [work[:, :128], work[:, 128:]]
    sub = lax.broadcasted_iota(jnp.int32, (STEP, 128), 0)
    for j in range(STEP):
        state = cols[j:] + data
        rows = [spread_row(x, j) for x in state]
        inverse = pltpu.reciprocal(rows[0], approx=False)
        factor = jnp.where(sub == j, 1.0 - inverse, cols[j] * inverse)
        state = [x - factor * r for x, r in zip(state, rows)]
        cols = cols[:j] + state[: STEP - j]
        data = state[STEP - j :]
    column = jnp.where(lane < row, -panel, panel)
    return jnp.concatenate(data, axis=1), column


def follow(rows, done, row):
    rel = lax.broadcasted_iota(jnp.int32, rows.shape, 1) - row
    t = row // 128
    cols = spread_lanes(lane_tile(rows, t), row - t * 128)
    rows = jnp.where((rel >= 0) & (rel < STEP), 0.0, rows)
    out = []
    for s in (0, 128):
        part = done[:, s : s + 128]
        terms = [cols[j] * spread_row(part, j) for j in range(STEP)]
        while len(terms) > 1:
            terms = [x + y for x, y in zip(terms[::2], terms[1::2])]
        out.append(rows[:, s : s + 128] - terms[0])
    return jnp.concatenate(out, axis=1)


def factors(left, right, column, done):
    c1, c2, c3 = split(column)
    r1, r2, r3 = split(done)
    left[...] = jnp.concatenate([c1, c1, c2, c2, c1, c3], axis=0).astype(bf16)
    right[...] = jnp.concatenate([r1, r2, r1, r2, r3, r1], axis=0).astype(bf16)


def late_update(a, left, right, row, done):
    update = lax.dot_general(
        left[...], right[...], CONTRACT_ROWS, preferred_element_type=f32
    )
    rel = lax.broadcasted_iota(jnp.int32, a.shape, 1) - row
    a[...] = jnp.where((rel >= 0) & (rel < STEP), 0.0, a[...]) - update
    a[pl.ds(row, STEP), :] = done


def invert(a, left, right, pauses):
    steps = a.shape[0] // STEP

    def at(k):
        return pl.multiple_of(k * STEP, STEP)

    done, column = pivot(a[0:STEP, :], 0)
    factors(left, right, column, done)
    panel = follow(a[STEP : 2 * STEP, :], done, 0)

    def body(k, carry):
        panel, before = carry
        late_update(a, left, right, at(k - 1), before)
        done, column = pivot(panel, at(k))
        panel = follow(a[pl.ds(at(k + 1), STEP), :], done, at(k))
        factors(left, right, column, done)
        return panel, done

    carry = (panel, done)
    first = 1
    for stop in sorted(pauses):
        carry = lax.fori_loop(first, stop, body, carry, unroll=2)
        pauses[stop]()
        first = stop
    panel, before = lax.fori_loop(first, steps - 1, body, carry, unroll=2)
    late_update(a, left, right, at(steps - 2), before)
    done, column = pivot(panel, at(steps - 1))
    factors(left, right, column, done)
    late_update(a, left, right, at(steps - 1), done)


def kernel(
    sizes,
    t_hbm,
    b_hbm,
    c_hbm,
    hf_ref,
    pf_ref,
    tbuf,
    con,
    cbuf,
    ct,
    bbuf,
    bt,
    gb_part,
    gb_in,
    gb_z,
    gc_part,
    gc_in,
    hmat,
    gcm,
    mht,
    mh,
    mh_in,
    mh_z,
    mhall,
    hft,
    hfall,
    mpt,
    mp,
    mp_in,
    owned,
    owned_in,
    left,
    right,
    lsem,
    ssem,
    rsem,
):
    NP, NH, NB = sizes
    Z, Q, NX = NP // 2, NH * NB, NH // 2
    hours, _, points = t_hbm.shape
    width = c_hbm.shape[1]
    half = width // 2
    prow = half // Q
    brow = b_hbm.shape[0]
    hh = hours // 2
    p, h, n = lax.axis_index("pts"), lax.axis_index("hrs"), lax.axis_index("bins")
    z, core = p // 2, lax.rem(p, 2)
    y_hi, x = h // NX, lax.rem(h, NX)
    q = h * NB + n
    g = 2 * core + n

    def plane(d):
        t = lax.rem(q + d, Q)
        return (p, t // NB, lax.rem(t, NB))

    def hour_block(d):
        flip = d // NX
        return (
            p,
            lax.rem(y_hi + flip, 2) * NX + lax.rem(x + d, NX),
            lax.rem(n + flip, 2),
        )

    def along_z(d):
        return (lax.rem(z + d, Z) * 2 + core, h, n)

    def quad(d):
        t = lax.rem(g + d, 4)
        return (z * 2 + t // 2, h, lax.rem(t, 2))

    other_core = (p + 1 - 2 * core, h, n)
    other_bins = (p, h, 1 - n)

    def remote(src, dst, i, target):
        return pltpu.make_async_remote_copy(
            src_ref=src,
            dst_ref=dst,
            send_sem=ssem.at[i],
            recv_sem=rsem.at[i],
            device_id=target,
            device_id_type=MESH,
        )

    def start_all(count, make, first=1):
        def body(d, _):
            make(d).start()
            return 0

        lax.fori_loop(first, count, body, 0)

    def wait_all(count, make, first=1):
        def body(d, _):
            make(d).wait()
            return 0

        lax.fori_loop(first, count, body, 0)

    def at(i, size):
        return pl.ds(pl.multiple_of(i * size, 8), size)

    base = 0

    def take(count):
        nonlocal base
        base += count
        return base - count

    my_b = at(h, brow)
    load_b = pltpu.make_async_copy(b_hbm, bbuf.at[my_b], lsem.at[hours])
    load_c = pltpu.make_async_copy(c_hbm, cbuf, lsem.at[hours + 1])
    load_b.start()
    load_c.start()

    def load_t(i):
        return pltpu.make_async_copy(t_hbm.at[i], tbuf.at[i], lsem.at[i])

    def start_t(i, _):
        load_t(i).start()
        return 0

    lax.fori_loop(0, hours, start_t, 0)

    barrier = pltpu.get_barrier_semaphore()

    def greet(make):
        def body(d, _):
            pl.semaphore_signal(
                barrier, inc=1, device_id=make(d), device_id_type=MESH
            )
            return 0

        return body

    lax.fori_loop(1, Q, greet(plane), 0)
    lax.fori_loop(1, Z, greet(along_z), 0)

    for device in (other_core, (p + 1 - 2 * core, h, 1 - n)):
        pl.semaphore_signal(barrier, inc=1, device_id=device, device_id_type=MESH)
    pl.semaphore_wait(barrier, Q - 1 + Z - 1 + 2)

    load_b.wait()
    b_base = take(NH)
    send_b = lambda d: remote(bbuf.at[my_b], bbuf.at[my_b], b_base + d, hour_block(d))
    start_all(NH, send_b)

    load_c.wait()
    chi, clo = halves(cbuf[...].T)
    ct[:width, :] = chi
    ct[width:, :] = clo

    chi, clo = ct[:width, :], ct[width:, :]
    mul = functools.partial(dot, dims=((1,), (1,)))
    gc_part[...] = mul(chi, chi) + (mul(chi, clo) + mul(clo, chi))
    my_half = at(core, half)
    send_gc = remote(gc_part.at[my_half], gc_in, take(1), other_bins)
    send_gc.start()

    group = 4

    def contract(i, _):
        for k in range(group):
            load_t(i * group + k).wait()
        for k in range(group):
            hour = i * group + k
            thi, tlo = halves(tbuf[hour])
            chi, clo = ct[:width, :], ct[width:, :]
            mul = functools.partial(dot, dims=((1,), (0,)))
            con[hour] = mul(chi, thi) + (mul(clo, thi) + mul(chi, tlo))
        return 0

    lax.fori_loop(0, hours // group, contract, 0)


    def add_up(ref, count):
        total = ref[0]
        for s in range(1, count):
            total = total + ref[s]
        return total

    wait_all(NH, send_b)
    gb_part[...] = gram(bbuf[...])
    my_rows = pl.ds(pl.multiple_of(half * core + prow * q, 8), prow)
    core_rows = pl.ds(pl.multiple_of(half * (1 - core) + prow * q, 8), prow)
    send_gb = remote(gb_part.at[core_rows], gb_in, take(1), other_core)
    send_gb.start()
    bt[...] = bbuf[...].T
    send_gb.wait()
    gb_z[z] = gb_part[my_rows, :] + gb_in[...]
    z_base = take(Z)
    send_gbz = lambda d: remote(gb_z.at[z], gb_z.at[z], z_base + d, along_z(d))
    start_all(Z, send_gbz)

    lane = lax.broadcasted_iota(jnp.int32, mht.shape, 1)

    def partial_hours(i, _):
        out = mht[...]
        for k in range(group):
            hour = i * group + k
            total = jnp.sum(con[hour] * bt[...], axis=1, keepdims=True)
            out = jnp.where(lane == hour, total, out)
        mht[...] = out
        return 0

    lax.fori_loop(0, hours // group, partial_hours, 0)
    mh[...] = mht[...].T[:hours, :]

    def tile(c2, n2):
        return at(c2, hh), pl.ds(pl.multiple_of(n2 * half, 128), half)

    my_tile = tile(core, n)
    mq_base = take(4)

    def send_mq(d):
        t = lax.rem(g + d, 4)
        return remote(
            mh.at[tile(t // 2, lax.rem(t, 2))], mh_in.at[g], mq_base + d, quad(d)
        )

    start_all(4, send_mq)
    mh_in[g] = mh[my_tile]
    mz_base = take(Z)
    send_mz = lambda d: remote(mh_z.at[z], mh_z.at[z], mz_base + d, along_z(d))
    my_hours = at(h, hours)
    ma_base = take(4)
    my_part = (
        pl.ds(pl.multiple_of(h * hours + core * hh, 8), hh),
        pl.ds(pl.multiple_of(n * half, 128), half),
    )
    send_ma = lambda d: remote(
        mhall.at[my_part], mhall.at[my_part], ma_base + d, quad(d)
    )
    mr_base = take(NH)
    send_mr = lambda d: remote(
        mhall.at[my_hours], mhall.at[my_hours], mr_base + d, hour_block(d)
    )

    wait_all(4, send_mq)
    mh_z[z] = add_up(mh_in, 4)
    start_all(Z, send_mz)

    wait_all(Z, send_gbz)
    send_gc.wait()
    gcm[my_half, :] = gc_part[my_half, :] + gc_in[...]
    swap_gc = remote(gcm.at[my_half], gcm.at[my_half], take(1), other_core)
    hmat[my_rows, :] = add_up(gb_z, Z) * gcm[my_rows, :]
    h_base = take(Q)
    send_h = lambda d: remote(hmat.at[my_rows], hmat.at[my_rows], h_base + d, plane(d))
    start_all(Q, send_h)
    swap_gc.start()

    wait_all(Z, send_mz)
    mhall[my_part] = add_up(mh_z, Z)
    start_all(4, send_ma)

    wait_all(Q, send_h)
    swap_h = remote(hmat.at[my_half], hmat.at[my_half], take(1), other_core)
    swap_h.start()
    wait_all(4, send_ma)
    start_all(NH, send_mr)
    swap_h.wait()
    invert(hmat, left, right, {})

    hour_rows = functools.partial(
        jnp.dot, precision=HIGHEST, preferred_element_type=f32
    )
    hf = hour_rows(mhall[my_hours, :], hmat[...])
    hft[...] = hf.T
    hf_ref[...] = hf

    mp_base = take(2 * NH)

    def send_mp(s):
        lanes = slice(s * half, (s + 1) * half)

        def make(d):
            flip = d // NX
            h2 = lax.rem(y_hi + flip, 2) * NX + lax.rem(x + d, NX)
            return remote(
                mp.at[at(h2, brow), lanes],
                mp_in.at[d, :, lanes],
                mp_base + s * NH + d,
                hour_block(d),
            )

        return make

    chunk = 32
    for s in range(2):
        for rows in range(s * half, (s + 1) * half, chunk):
            weights = hft[rows : rows + chunk, :]
            acc = con[0, rows : rows + chunk, :] * weights[:, 0:1]
            for i in range(1, hours):
                acc = acc + con[i, rows : rows + chunk, :] * weights[:, i : i + 1]
            mpt[rows : rows + chunk, :] = acc
        lanes = slice(s * half, (s + 1) * half)
        mp[:, lanes] = mpt[lanes, :].T
        start_all(NH, send_mp(s))

    wait_all(NH, send_mr)
    swap_gc.wait()
    hfall[...] = hour_rows(mhall[...], hmat[...])
    hmat[...] = gram(hfall[...]) * gcm[...]
    swap_o = remote(owned, owned_in, take(1), other_bins)

    def pause_points():
        wait_all(NH, send_mp(0))
        wait_all(NH, send_mp(1))
        total = mp[my_b, :]
        for s in range(1, NH):
            total = total + mp_in[s]
        owned[...] = total
        swap_o.start()

    invert(hmat, left, right, {13: pause_points})
    swap_o.wait()
    pf_ref[...] = jnp.dot(
        owned[...] + owned_in[...],
        hmat[...],
        precision=HIGHEST,
        preferred_element_type=f32,
    )


def local(sizes, tensor, b_factor, c_factor):
    NP, NH, NB = sizes
    Z, Q = NP // 2, NH * NB
    tensor = jnp.swapaxes(tensor, 1, 2)
    hours, bins, points = tensor.shape
    width = c_factor.shape[1]
    brow = b_factor.shape[0]
    prow = width // (2 * Q)
    hh = hours // 2
    sems = 2 * Z + Q + 4 * NH + 8 + 6
    vm = lambda *shape: pltpu.VMEM(shape, f32)
    any_spec = pl.BlockSpec(memory_space=pltpu.HBM)
    vmem_spec = pl.BlockSpec(memory_space=pltpu.VMEM)
    out_shape = (
        jax.ShapeDtypeStruct((hours, width), f32),
        jax.ShapeDtypeStruct((brow, width), f32),
    )
    return pl.pallas_call(
        functools.partial(kernel, sizes),
        out_shape=out_shape,
        in_specs=[any_spec] * 3,
        out_specs=(vmem_spec, vmem_spec),
        scratch_shapes=[
            vm(hours, bins, points),
            vm(hours, width, points),
            vm(bins, width),
            pltpu.VMEM((2 * width, bins), bf16),
            vm(points, width),
            vm(width, points),
            vm(width, width),
            vm(prow, width),
            vm(Z, prow, width),
            vm(width, width),
            vm(width // 2, width),
            vm(width, width),
            vm(width, width),
            vm(width, 128),
            vm(hours, width),
            vm(4, hh, width // 2),
            vm(Z, hh, width // 2),
            vm(hours * NH, width),
            vm(width, hours),
            vm(hours * NH, width),
            vm(width, points),
            vm(points, width),
            vm(NH, brow, width),
            vm(brow, width),
            vm(brow, width),
            pltpu.VMEM((6 * STEP, width), bf16),
            pltpu.VMEM((6 * STEP, width), bf16),
            pltpu.SemaphoreType.DMA((hours + 2,)),
            pltpu.SemaphoreType.DMA((sems,)),
            pltpu.SemaphoreType.DMA((sems,)),
        ],
        compiler_params=pltpu.CompilerParams(
            collective_id=0,
            has_side_effects=True,
            vmem_limit_bytes=55160 * 1024,
        ),
    )(tensor, b_factor, c_factor)


def solution(mesh):
    sizes = (mesh.shape["pts"], mesh.shape["hrs"], mesh.shape["bins"])
    placed = (P("hrs", "pts", "bins"), P(("pts", "hrs"), None), P("bins", None))
    return jax.shard_map(
        functools.partial(local, sizes),
        mesh=mesh,
        in_specs=placed,
        out_specs=(P("hrs", None), P(("pts", "hrs"), None)),
        check_vma=False,
    )
```

```python
import functools

import jax
import jax.numpy as jnp
from jax import lax
from jax.experimental import pallas as pl
from jax.experimental.pallas import tpu as pltpu
from jax.sharding import PartitionSpec as P

f32 = jnp.float32
bf16 = jnp.bfloat16
HIGHEST = lax.Precision.HIGHEST
MESH = pl.DeviceIdType.MESH
CONTRACT_ROWS = (((0,), (0,)), ((), ()))


def dot(a, b, dims):
    return lax.dot_general(a, b, (dims, ((), ())), preferred_element_type=f32)


def halves(x):
    hi = x.astype(bf16)
    return hi, (x - hi.astype(f32)).astype(bf16)


def gram(x):
    hi = x.astype(bf16).astype(f32)
    lo = x - hi
    left = jnp.concatenate([hi, hi, lo], axis=0).astype(bf16)
    right = jnp.concatenate([hi, lo, hi], axis=0).astype(bf16)
    return dot(left, right, ((0,), (0,)))


def split(x):
    first = x.astype(bf16).astype(f32)
    rest = x - first
    second = rest.astype(bf16).astype(f32)
    return first, second, rest - second


STEP = 16


def spread_lanes(x, first):
    return [
        jnp.take_along_axis(
            x,
            jnp.full(x.shape, first + j, jnp.int32),
            axis=1,
            mode="promise_in_bounds",
        )
        for j in range(STEP)
    ]


def spread_row(x, j):
    return jnp.broadcast_to(x[j : j + 1, :], x.shape)


def lane_tile(x, t):
    return jnp.where(t == 0, x[:, :128], x[:, 128:])


def pivot(panel, row):
    lane = lax.broadcasted_iota(jnp.int32, panel.shape, 1)
    sub = lax.broadcasted_iota(jnp.int32, panel.shape, 0)
    rel = lane - row
    t = row // 128
    cols = spread_lanes(lane_tile(panel, t), row - t * 128)
    work = jnp.where((rel >= 0) & (rel < STEP), jnp.where(rel == sub, 1.0, 0.0), panel)
    data = [work[:, :128], work[:, 128:]]
    sub = lax.broadcasted_iota(jnp.int32, (STEP, 128), 0)
    for j in range(STEP):
        state = cols[j:] + data
        rows = [spread_row(x, j) for x in state]
        inverse = pltpu.reciprocal(rows[0], approx=False)
        factor = jnp.where(sub == j, 1.0 - inverse, cols[j] * inverse)
        state = [x - factor * r for x, r in zip(state, rows)]
        cols = cols[:j] + state[: STEP - j]
        data = state[STEP - j :]
    column = jnp.where(lane < row, -panel, panel)
    return jnp.concatenate(data, axis=1), column


def follow(rows, done, row):
    rel = lax.broadcasted_iota(jnp.int32, rows.shape, 1) - row
    t = row // 128
    cols = spread_lanes(lane_tile(rows, t), row - t * 128)
    rows = jnp.where((rel >= 0) & (rel < STEP), 0.0, rows)
    out = []
    for s in (0, 128):
        part = done[:, s : s + 128]
        terms = [cols[j] * spread_row(part, j) for j in range(STEP)]
        while len(terms) > 1:
            terms = [x + y for x, y in zip(terms[::2], terms[1::2])]
        out.append(rows[:, s : s + 128] - terms[0])
    return jnp.concatenate(out, axis=1)


def factors(left, right, column, done):
    c1, c2, c3 = split(column)
    r1, r2, r3 = split(done)
    left[...] = jnp.concatenate([c1, c1, c2, c2, c1, c3], axis=0).astype(bf16)
    right[...] = jnp.concatenate([r1, r2, r1, r2, r3, r1], axis=0).astype(bf16)


def late_update(a, left, right, row, done):
    update = lax.dot_general(
        left[...], right[...], CONTRACT_ROWS, preferred_element_type=f32
    )
    rel = lax.broadcasted_iota(jnp.int32, a.shape, 1) - row
    a[...] = jnp.where((rel >= 0) & (rel < STEP), 0.0, a[...]) - update
    a[pl.ds(row, STEP), :] = done


def invert(a, left, right, pauses, unroll):
    steps = a.shape[0] // STEP

    def at(k):
        return pl.multiple_of(k * STEP, STEP)

    done, column = pivot(a[0:STEP, :], 0)
    factors(left, right, column, done)
    panel = follow(a[STEP : 2 * STEP, :], done, 0)

    def body(k, carry):
        panel, before = carry
        late_update(a, left, right, at(k - 1), before)
        done, column = pivot(panel, at(k))
        panel = follow(a[pl.ds(at(k + 1), STEP), :], done, at(k))
        factors(left, right, column, done)
        return panel, done

    carry = (panel, done)
    first = 1
    for stop in sorted(pauses):
        carry = lax.fori_loop(first, stop, body, carry, unroll=unroll)
        pauses[stop]()
        first = stop
    panel, before = lax.fori_loop(first, steps - 1, body, carry, unroll=unroll)
    late_update(a, left, right, at(steps - 2), before)
    done, column = pivot(panel, at(steps - 1))
    factors(left, right, column, done)
    late_update(a, left, right, at(steps - 1), done)


def kernel(
    sizes,
    t_hbm,
    b_hbm,
    c_hbm,
    hf_ref,
    pf_ref,
    tbuf,
    con,
    cbuf,
    ct,
    bbuf,
    bt,
    gb_part,
    gb_in,
    gb_z,
    gc_part,
    gc_in,
    hmat,
    gcm,
    mht,
    mh,
    mh_in,
    mh_z,
    mhall,
    hft,
    hfall,
    mpt,
    mp,
    mp_in,
    owned,
    owned_in,
    left,
    right,
    lsem,
    ssem,
    rsem,
):
    NP, NH, NB = sizes
    Z, Q, NX = NP // 2, NH * NB, NH // 2
    hours, _, points = t_hbm.shape
    width = c_hbm.shape[1]
    half = width // 2
    prow = half // Q
    brow = b_hbm.shape[0]
    hh = hours // 2
    p, h, n = lax.axis_index("pts"), lax.axis_index("hrs"), lax.axis_index("bins")
    z, core = p // 2, lax.rem(p, 2)
    y_hi, x = h // NX, lax.rem(h, NX)
    q = h * NB + n
    g = 2 * core + n

    def plane(d):
        t = lax.rem(q + d, Q)
        return (p, t // NB, lax.rem(t, NB))

    def hour_block(d):
        flip = d // NX
        return (
            p,
            lax.rem(y_hi + flip, 2) * NX + lax.rem(x + d, NX),
            lax.rem(n + flip, 2),
        )

    def along_z(d):
        return (lax.rem(z + d, Z) * 2 + core, h, n)

    def quad(d):
        t = lax.rem(g + d, 4)
        return (z * 2 + t // 2, h, lax.rem(t, 2))

    other_core = (p + 1 - 2 * core, h, n)
    other_bins = (p, h, 1 - n)

    def remote(src, dst, i, target):
        return pltpu.make_async_remote_copy(
            src_ref=src,
            dst_ref=dst,
            send_sem=ssem.at[i],
            recv_sem=rsem.at[i],
            device_id=target,
            device_id_type=MESH,
        )

    def start_all(count, make, first=1):
        def body(d, _):
            make(d).start()
            return 0

        lax.fori_loop(first, count, body, 0)

    def wait_all(count, make, first=1):
        def body(d, _):
            make(d).wait()
            return 0

        lax.fori_loop(first, count, body, 0)

    def at(i, size):
        return pl.ds(pl.multiple_of(i * size, 8), size)

    base = 0

    def take(count):
        nonlocal base
        base += count
        return base - count

    my_b = at(h, brow)
    load_b = pltpu.make_async_copy(b_hbm, bbuf.at[my_b], lsem.at[hours])
    load_c = pltpu.make_async_copy(c_hbm, cbuf, lsem.at[hours + 1])
    load_b.start()

    def load_t(i):
        return pltpu.make_async_copy(t_hbm.at[i], tbuf.at[i], lsem.at[i])

    def start_t(i, _):
        load_t(i).start()
        return 0

    barrier = pltpu.get_barrier_semaphore()

    def greet(make):
        def body(d, _):
            pl.semaphore_signal(
                barrier, inc=1, device_id=make(d), device_id_type=MESH
            )
            return 0

        return body

    lax.fori_loop(1, Q, greet(plane), 0)
    lax.fori_loop(1, Z, greet(along_z), 0)

    for device in (other_core, (p + 1 - 2 * core, h, 1 - n)):
        pl.semaphore_signal(barrier, inc=1, device_id=device, device_id_type=MESH)
    load_c.start()
    lax.fori_loop(0, hours, start_t, 0)
    pl.semaphore_wait(barrier, Q - 1 + Z - 1 + 2)

    load_b.wait()
    b_base = take(NH)
    send_b = lambda d: remote(bbuf.at[my_b], bbuf.at[my_b], b_base + d, hour_block(d))
    start_all(NH, send_b)

    load_c.wait()
    chi, clo = halves(cbuf[...].T)
    ct[:width, :] = chi
    ct[width:, :] = clo

    chi, clo = ct[:width, :], ct[width:, :]
    mul = functools.partial(dot, dims=((1,), (1,)))
    gc_part[...] = mul(chi, chi) + (mul(chi, clo) + mul(clo, chi))
    my_half = at(core, half)
    send_gc = remote(gc_part.at[my_half], gc_in, take(1), other_bins)
    send_gc.start()

    group = 4

    def contract(i, _):
        for k in range(group):
            load_t(i * group + k).wait()
        for k in range(group):
            hour = i * group + k
            thi, tlo = halves(tbuf[hour])
            chi, clo = ct[:width, :], ct[width:, :]
            mul = functools.partial(dot, dims=((1,), (0,)))
            con[hour] = mul(chi, thi) + (mul(clo, thi) + mul(chi, tlo))
        return 0

    lax.fori_loop(0, hours // group, contract, 0)


    def add_up(ref, count):
        total = ref[0]
        for s in range(1, count):
            total = total + ref[s]
        return total

    wait_all(NH, send_b)
    gb_part[...] = gram(bbuf[...])
    my_rows = pl.ds(pl.multiple_of(half * core + prow * q, 8), prow)
    core_rows = pl.ds(pl.multiple_of(half * (1 - core) + prow * q, 8), prow)
    send_gb = remote(gb_part.at[core_rows], gb_in, take(1), other_core)
    send_gb.start()
    bt[...] = bbuf[...].T
    send_gb.wait()
    gb_z[z] = gb_part[my_rows, :] + gb_in[...]
    z_base = take(Z)
    send_gbz = lambda d: remote(gb_z.at[z], gb_z.at[z], z_base + d, along_z(d))
    start_all(Z, send_gbz)

    lane = lax.broadcasted_iota(jnp.int32, mht.shape, 1)

    def partial_hours(i, _):
        out = mht[...]
        for k in range(group):
            hour = i * group + k
            total = jnp.sum(con[hour] * bt[...], axis=1, keepdims=True)
            out = jnp.where(lane == hour, total, out)
        mht[...] = out
        return 0

    lax.fori_loop(0, hours // group, partial_hours, 0)
    mh[...] = mht[...].T[:hours, :]

    def tile(c2, n2):
        return at(c2, hh), pl.ds(pl.multiple_of(n2 * half, 128), half)

    my_tile = tile(core, n)
    mq_base = take(4)

    def send_mq(d):
        t = lax.rem(g + d, 4)
        return remote(
            mh.at[tile(t // 2, lax.rem(t, 2))], mh_in.at[g], mq_base + d, quad(d)
        )

    start_all(4, send_mq)
    mh_in[g] = mh[my_tile]
    mz_base = take(Z)
    send_mz = lambda d: remote(mh_z.at[z], mh_z.at[z], mz_base + d, along_z(d))
    my_hours = at(h, hours)
    ma_base = take(4)
    my_part = (
        pl.ds(pl.multiple_of(h * hours + core * hh, 8), hh),
        pl.ds(pl.multiple_of(n * half, 128), half),
    )
    send_ma = lambda d: remote(
        mhall.at[my_part], mhall.at[my_part], ma_base + d, quad(d)
    )
    mr_base = take(NH)
    send_mr = lambda d: remote(
        mhall.at[my_hours], mhall.at[my_hours], mr_base + d, hour_block(d)
    )

    wait_all(4, send_mq)
    mh_z[z] = add_up(mh_in, 4)
    start_all(Z, send_mz)

    wait_all(Z, send_gbz)
    send_gc.wait()
    gcm[my_half, :] = gc_part[my_half, :] + gc_in[...]
    swap_gc = remote(gcm.at[my_half], gcm.at[my_half], take(1), other_core)
    hmat[my_rows, :] = add_up(gb_z, Z) * gcm[my_rows, :]
    h_base = take(Q)
    send_h = lambda d: remote(hmat.at[my_rows], hmat.at[my_rows], h_base + d, plane(d))
    start_all(Q, send_h)
    swap_gc.start()

    wait_all(Z, send_mz)
    mhall[my_part] = add_up(mh_z, Z)
    start_all(4, send_ma)

    wait_all(Q, send_h)
    swap_h = remote(hmat.at[my_half], hmat.at[my_half], take(1), other_core)
    swap_h.start()
    wait_all(4, send_ma)
    start_all(NH, send_mr)
    swap_h.wait()
    invert(hmat, left, right, {}, 7)

    hour_rows = functools.partial(
        jnp.dot, precision=HIGHEST, preferred_element_type=f32
    )
    hf = hour_rows(mhall[my_hours, :], hmat[...])
    hft[...] = hf.T
    hf_ref[...] = hf

    mp_base = take(2 * NH)

    def send_mp(s):
        lanes = slice(s * half, (s + 1) * half)

        def make(d):
            flip = d // NX
            h2 = lax.rem(y_hi + flip, 2) * NX + lax.rem(x + d, NX)
            return remote(
                mp.at[at(h2, brow), lanes],
                mp_in.at[d, :, lanes],
                mp_base + s * NH + d,
                hour_block(d),
            )

        return make

    chunk = 32
    for s in range(2):
        for rows in range(s * half, (s + 1) * half, chunk):
            weights = hft[rows : rows + chunk, :]
            acc = con[0, rows : rows + chunk, :] * weights[:, 0:1]
            for i in range(1, hours):
                acc = acc + con[i, rows : rows + chunk, :] * weights[:, i : i + 1]
            mpt[rows : rows + chunk, :] = acc
        lanes = slice(s * half, (s + 1) * half)
        mp[:, lanes] = mpt[lanes, :].T
        start_all(NH, send_mp(s))

    wait_all(NH, send_mr)
    swap_gc.wait()
    hfall[...] = hour_rows(mhall[...], hmat[...])
    hmat[...] = gram(hfall[...]) * gcm[...]
    o_base = take(2)

    def swap_o(s):
        lanes = slice(s * half, (s + 1) * half)
        return remote(owned.at[:, lanes], owned_in.at[:, lanes], o_base + s, other_bins)

    def pause_points(s):
        lanes = slice(s * half, (s + 1) * half)

        def pause():
            wait_all(NH, send_mp(s))
            total = mp[my_b, lanes]
            for d in range(1, NH):
                total = total + mp_in[d, :, lanes]
            owned[:, lanes] = total
            swap_o(s).start()

        return pause

    invert(hmat, left, right, {9: pause_points(0), 13: pause_points(1)}, 2)
    swap_o(0).wait()
    swap_o(1).wait()
    pf_ref[...] = jnp.dot(
        owned[...] + owned_in[...],
        hmat[...],
        precision=HIGHEST,
        preferred_element_type=f32,
    )


def local(sizes, tensor, b_factor, c_factor):
    NP, NH, NB = sizes
    Z, Q = NP // 2, NH * NB
    tensor = jnp.swapaxes(tensor, 1, 2)
    hours, bins, points = tensor.shape
    width = c_factor.shape[1]
    brow = b_factor.shape[0]
    prow = width // (2 * Q)
    hh = hours // 2
    sems = 2 * Z + Q + 4 * NH + 8 + 6
    vm = lambda *shape: pltpu.VMEM(shape, f32)
    any_spec = pl.BlockSpec(memory_space=pltpu.HBM)
    vmem_spec = pl.BlockSpec(memory_space=pltpu.VMEM)
    out_shape = (
        jax.ShapeDtypeStruct((hours, width), f32),
        jax.ShapeDtypeStruct((brow, width), f32),
    )
    return pl.pallas_call(
        functools.partial(kernel, sizes),
        out_shape=out_shape,
        in_specs=[any_spec] * 3,
        out_specs=(vmem_spec, vmem_spec),
        scratch_shapes=[
            vm(hours, bins, points),
            vm(hours, width, points),
            vm(bins, width),
            pltpu.VMEM((2 * width, bins), bf16),
            vm(points, width),
            vm(width, points),
            vm(width, width),
            vm(prow, width),
            vm(Z, prow, width),
            vm(width, width),
            vm(width // 2, width),
            vm(width, width),
            vm(width, width),
            vm(width, 128),
            vm(hours, width),
            vm(4, hh, width // 2),
            vm(Z, hh, width // 2),
            vm(hours * NH, width),
            vm(width, hours),
            vm(hours * NH, width),
            vm(width, points),
            vm(points, width),
            vm(NH, brow, width),
            vm(brow, width),
            vm(brow, width),
            pltpu.VMEM((6 * STEP, width), bf16),
            pltpu.VMEM((6 * STEP, width), bf16),
            pltpu.SemaphoreType.DMA((hours + 2,)),
            pltpu.SemaphoreType.DMA((sems,)),
            pltpu.SemaphoreType.DMA((sems,)),
        ],
        compiler_params=pltpu.CompilerParams(
            collective_id=0,
            has_side_effects=True,
            vmem_limit_bytes=55160 * 1024,
        ),
    )(tensor, b_factor, c_factor)


def solution(mesh):
    sizes = (mesh.shape["pts"], mesh.shape["hrs"], mesh.shape["bins"])
    placed = (P("hrs", "pts", "bins"), P(("pts", "hrs"), None), P("bins", None))
    return jax.shard_map(
        functools.partial(local, sizes),
        mesh=mesh,
        in_specs=placed,
        out_specs=(P("hrs", None), P(("pts", "hrs"), None)),
        check_vma=False,
    )
```

```python
import functools

import jax
import jax.numpy as jnp
from jax import lax
from jax.experimental import pallas as pl
from jax.experimental.pallas import tpu as pltpu
from jax.sharding import PartitionSpec as P

f32 = jnp.float32
bf16 = jnp.bfloat16
HIGHEST = lax.Precision.HIGHEST
MESH = pl.DeviceIdType.MESH
CONTRACT_ROWS = (((0,), (0,)), ((), ()))


def dot(a, b, dims):
    return lax.dot_general(a, b, (dims, ((), ())), preferred_element_type=f32)


def halves(x):
    hi = x.astype(bf16)
    return hi, (x - hi.astype(f32)).astype(bf16)


def gram(x):
    hi = x.astype(bf16).astype(f32)
    lo = x - hi
    left = jnp.concatenate([hi, hi, lo], axis=0).astype(bf16)
    right = jnp.concatenate([hi, lo, hi], axis=0).astype(bf16)
    return dot(left, right, ((0,), (0,)))


def split(x):
    first = x.astype(bf16).astype(f32)
    rest = x - first
    second = rest.astype(bf16).astype(f32)
    return first, second, rest - second


STEP = 16


def spread_lanes(x, first):
    return [
        jnp.take_along_axis(
            x,
            jnp.full(x.shape, first + j, jnp.int32),
            axis=1,
            mode="promise_in_bounds",
        )
        for j in range(STEP)
    ]


def spread_row(x, j):
    return jnp.broadcast_to(x[j : j + 1, :], x.shape)


def lane_tile(x, t):
    return jnp.where(t == 0, x[:, :128], x[:, 128:])


def pivot(panel, row):
    lane = lax.broadcasted_iota(jnp.int32, panel.shape, 1)
    sub = lax.broadcasted_iota(jnp.int32, panel.shape, 0)
    rel = lane - row
    t = row // 128
    cols = spread_lanes(lane_tile(panel, t), row - t * 128)
    work = jnp.where((rel >= 0) & (rel < STEP), jnp.where(rel == sub, 1.0, 0.0), panel)
    data = [work[:, :128], work[:, 128:]]
    sub = lax.broadcasted_iota(jnp.int32, (STEP, 128), 0)
    for j in range(STEP):
        state = cols[j:] + data
        rows = [spread_row(x, j) for x in state]
        inverse = pltpu.reciprocal(rows[0], approx=False)
        factor = jnp.where(sub == j, 1.0 - inverse, cols[j] * inverse)
        state = [x - factor * r for x, r in zip(state, rows)]
        cols = cols[:j] + state[: STEP - j]
        data = state[STEP - j :]
    column = jnp.where(lane < row, -panel, panel)
    return jnp.concatenate(data, axis=1), column


def follow(rows, done, row):
    rel = lax.broadcasted_iota(jnp.int32, rows.shape, 1) - row
    t = row // 128
    cols = spread_lanes(lane_tile(rows, t), row - t * 128)
    rows = jnp.where((rel >= 0) & (rel < STEP), 0.0, rows)
    out = []
    for s in (0, 128):
        part = done[:, s : s + 128]
        terms = [cols[j] * spread_row(part, j) for j in range(STEP)]
        while len(terms) > 1:
            terms = [x + y for x, y in zip(terms[::2], terms[1::2])]
        out.append(rows[:, s : s + 128] - terms[0])
    return jnp.concatenate(out, axis=1)


def factors(left, right, column, done):
    c1, c2, c3 = split(column)
    r1, r2, r3 = split(done)
    left[...] = jnp.concatenate([c1, c1, c2, c2, c1, c3], axis=0).astype(bf16)
    right[...] = jnp.concatenate([r1, r2, r1, r2, r3, r1], axis=0).astype(bf16)


def late_update(a, left, right, row, done):
    update = lax.dot_general(
        left[...], right[...], CONTRACT_ROWS, preferred_element_type=f32
    )
    rel = lax.broadcasted_iota(jnp.int32, a.shape, 1) - row
    a[...] = jnp.where((rel >= 0) & (rel < STEP), 0.0, a[...]) - update
    a[pl.ds(row, STEP), :] = done


def invert(a, left, right, pauses, unroll):
    steps = a.shape[0] // STEP

    def at(k):
        return pl.multiple_of(k * STEP, STEP)

    done, column = pivot(a[0:STEP, :], 0)
    factors(left, right, column, done)
    panel = follow(a[STEP : 2 * STEP, :], done, 0)

    def body(k, carry):
        panel, before = carry
        late_update(a, left, right, at(k - 1), before)
        done, column = pivot(panel, at(k))
        panel = follow(a[pl.ds(at(k + 1), STEP), :], done, at(k))
        factors(left, right, column, done)
        return panel, done

    carry = (panel, done)
    first = 1
    for stop in sorted(pauses):
        carry = lax.fori_loop(first, stop, body, carry, unroll=unroll)
        pauses[stop]()
        first = stop
    panel, before = lax.fori_loop(first, steps - 1, body, carry, unroll=unroll)
    late_update(a, left, right, at(steps - 2), before)
    done, column = pivot(panel, at(steps - 1))
    factors(left, right, column, done)
    late_update(a, left, right, at(steps - 1), done)


def kernel(
    sizes,
    t_hbm,
    b_hbm,
    c_hbm,
    hf_ref,
    pf_ref,
    tbuf,
    con,
    cbuf,
    ct,
    bbuf,
    bt,
    gb_part,
    gb_in,
    gb_z,
    gc_part,
    gc_in,
    hmat,
    gcm,
    mht,
    mh,
    mh_in,
    mh_z,
    mhall,
    hft,
    hfall,
    mpt,
    mp,
    mp_in,
    owned,
    owned_in,
    left,
    right,
    lsem,
    ssem,
    rsem,
):
    NP, NH, NB = sizes
    Z, Q, NX = NP // 2, NH * NB, NH // 2
    hours, _, points = t_hbm.shape
    width = c_hbm.shape[1]
    half = width // 2
    prow = half // Q
    brow = b_hbm.shape[0]
    hh = hours // 2
    p, h, n = lax.axis_index("pts"), lax.axis_index("hrs"), lax.axis_index("bins")
    z, core = p // 2, lax.rem(p, 2)
    y_hi, x = h // NX, lax.rem(h, NX)
    q = h * NB + n
    g = 2 * core + n

    def plane(d):
        t = lax.rem(q + d, Q)
        return (p, t // NB, lax.rem(t, NB))

    def hour_block(d):
        flip = d // NX
        return (
            p,
            lax.rem(y_hi + flip, 2) * NX + lax.rem(x + d, NX),
            lax.rem(n + flip, 2),
        )

    def along_z(d):
        return (lax.rem(z + d, Z) * 2 + core, h, n)

    def quad(d):
        t = lax.rem(g + d, 4)
        return (z * 2 + t // 2, h, lax.rem(t, 2))

    other_core = (p + 1 - 2 * core, h, n)
    other_bins = (p, h, 1 - n)

    def remote(src, dst, i, target):
        return pltpu.make_async_remote_copy(
            src_ref=src,
            dst_ref=dst,
            send_sem=ssem.at[i],
            recv_sem=rsem.at[i],
            device_id=target,
            device_id_type=MESH,
        )

    def start_all(count, make, first=1):
        def body(d, _):
            make(d).start()
            return 0

        lax.fori_loop(first, count, body, 0)

    def start_far_first(count, make, ring):
        def distance(d):
            return min(d % ring, ring - d % ring)

        for d in sorted(range(1, count), key=distance, reverse=True):
            make(d).start()

    def wait_all(count, make, first=1):
        def body(d, _):
            make(d).wait()
            return 0

        lax.fori_loop(first, count, body, 0)

    def at(i, size):
        return pl.ds(pl.multiple_of(i * size, 8), size)

    base = 0

    def take(count):
        nonlocal base
        base += count
        return base - count

    my_b = at(h, brow)
    load_b = pltpu.make_async_copy(b_hbm, bbuf.at[my_b], lsem.at[hours])
    load_c = pltpu.make_async_copy(c_hbm, cbuf, lsem.at[hours + 1])
    load_b.start()

    def load_t(i):
        return pltpu.make_async_copy(t_hbm.at[i], tbuf.at[i], lsem.at[i])

    def start_t(i, _):
        load_t(i).start()
        return 0

    barrier = pltpu.get_barrier_semaphore()

    def greet(make):
        def body(d, _):
            pl.semaphore_signal(
                barrier, inc=1, device_id=make(d), device_id_type=MESH
            )
            return 0

        return body

    lax.fori_loop(1, Q, greet(plane), 0)
    lax.fori_loop(1, Z, greet(along_z), 0)

    for device in (other_core, (p + 1 - 2 * core, h, 1 - n)):
        pl.semaphore_signal(barrier, inc=1, device_id=device, device_id_type=MESH)
    load_c.start()
    lax.fori_loop(0, hours, start_t, 0)
    pl.semaphore_wait(barrier, Q - 1 + Z - 1 + 2)

    load_b.wait()
    b_base = take(NH)
    send_b = lambda d: remote(bbuf.at[my_b], bbuf.at[my_b], b_base + d, hour_block(d))
    start_far_first(NH, send_b, NX)

    load_c.wait()
    chi, clo = halves(cbuf[...].T)
    ct[:width, :] = chi
    ct[width:, :] = clo

    chi, clo = ct[:width, :], ct[width:, :]
    mul = functools.partial(dot, dims=((1,), (1,)))
    gc_part[...] = mul(chi, chi) + (mul(chi, clo) + mul(clo, chi))
    my_half = at(core, half)
    send_gc = remote(gc_part.at[my_half], gc_in, take(1), other_bins)
    send_gc.start()

    group = 4

    def contract(i, _):
        for k in range(group):
            load_t(i * group + k).wait()
        for k in range(group):
            hour = i * group + k
            thi, tlo = halves(tbuf[hour])
            chi, clo = ct[:width, :], ct[width:, :]
            mul = functools.partial(dot, dims=((1,), (0,)))
            con[hour] = mul(chi, thi) + (mul(clo, thi) + mul(chi, tlo))
        return 0

    lax.fori_loop(0, hours // group, contract, 0)


    def add_up(ref, count):
        total = ref[0]
        for s in range(1, count):
            total = total + ref[s]
        return total

    wait_all(NH, send_b)
    gb_part[...] = gram(bbuf[...])
    my_rows = pl.ds(pl.multiple_of(half * core + prow * q, 8), prow)
    core_rows = pl.ds(pl.multiple_of(half * (1 - core) + prow * q, 8), prow)
    send_gb = remote(gb_part.at[core_rows], gb_in, take(1), other_core)
    send_gb.start()
    bt[...] = bbuf[...].T
    send_gb.wait()
    gb_z[z] = gb_part[my_rows, :] + gb_in[...]
    z_base = take(Z)
    send_gbz = lambda d: remote(gb_z.at[z], gb_z.at[z], z_base + d, along_z(d))
    start_far_first(Z, send_gbz, Z)

    lane = lax.broadcasted_iota(jnp.int32, mht.shape, 1)

    def partial_hours(i, _):
        out = mht[...]
        for k in range(group):
            hour = i * group + k
            total = jnp.sum(con[hour] * bt[...], axis=1, keepdims=True)
            out = jnp.where(lane == hour, total, out)
        mht[...] = out
        return 0

    lax.fori_loop(0, hours // group, partial_hours, 0)
    mh[...] = mht[...].T[:hours, :]

    def tile(c2, n2):
        return at(c2, hh), pl.ds(pl.multiple_of(n2 * half, 128), half)

    my_tile = tile(core, n)
    mq_base = take(4)

    def send_mq(d):
        t = lax.rem(g + d, 4)
        return remote(
            mh.at[tile(t // 2, lax.rem(t, 2))], mh_in.at[g], mq_base + d, quad(d)
        )

    start_all(4, send_mq)
    mh_in[g] = mh[my_tile]
    mz_base = take(Z)
    send_mz = lambda d: remote(mh_z.at[z], mh_z.at[z], mz_base + d, along_z(d))
    my_hours = at(h, hours)
    ma_base = take(4)
    my_part = (
        pl.ds(pl.multiple_of(h * hours + core * hh, 8), hh),
        pl.ds(pl.multiple_of(n * half, 128), half),
    )
    send_ma = lambda d: remote(
        mhall.at[my_part], mhall.at[my_part], ma_base + d, quad(d)
    )
    mr_base = take(NH)
    send_mr = lambda d: remote(
        mhall.at[my_hours], mhall.at[my_hours], mr_base + d, hour_block(d)
    )

    wait_all(4, send_mq)
    mh_z[z] = add_up(mh_in, 4)
    start_far_first(Z, send_mz, Z)

    wait_all(Z, send_gbz)
    send_gc.wait()
    gcm[my_half, :] = gc_part[my_half, :] + gc_in[...]
    swap_gc = remote(gcm.at[my_half], gcm.at[my_half], take(1), other_core)
    hmat[my_rows, :] = add_up(gb_z, Z) * gcm[my_rows, :]
    h_base = take(Q)
    send_h = lambda d: remote(hmat.at[my_rows], hmat.at[my_rows], h_base + d, plane(d))
    start_all(Q, send_h)
    swap_gc.start()

    wait_all(Z, send_mz)
    mhall[my_part] = add_up(mh_z, Z)
    start_all(4, send_ma)

    wait_all(Q, send_h)
    swap_h = remote(hmat.at[my_half], hmat.at[my_half], take(1), other_core)
    swap_h.start()
    wait_all(4, send_ma)
    start_far_first(NH, send_mr, NX)
    swap_h.wait()
    invert(hmat, left, right, {}, 7)

    hour_rows = functools.partial(
        jnp.dot, precision=HIGHEST, preferred_element_type=f32
    )
    hf = hour_rows(mhall[my_hours, :], hmat[...])
    hft[...] = hf.T
    hf_ref[...] = hf

    mp_base = take(2 * NH)

    def send_mp(s):
        lanes = slice(s * half, (s + 1) * half)

        def make(d):
            flip = d // NX
            h2 = lax.rem(y_hi + flip, 2) * NX + lax.rem(x + d, NX)
            return remote(
                mp.at[at(h2, brow), lanes],
                mp_in.at[d, :, lanes],
                mp_base + s * NH + d,
                hour_block(d),
            )

        return make

    chunk = 32
    for s in range(2):
        for rows in range(s * half, (s + 1) * half, chunk):
            weights = hft[rows : rows + chunk, :]
            acc = con[0, rows : rows + chunk, :] * weights[:, 0:1]
            for i in range(1, hours):
                acc = acc + con[i, rows : rows + chunk, :] * weights[:, i : i + 1]
            mpt[rows : rows + chunk, :] = acc
        lanes = slice(s * half, (s + 1) * half)
        mp[:, lanes] = mpt[lanes, :].T
        start_far_first(NH, send_mp(s), NX)

    wait_all(NH, send_mr)
    swap_gc.wait()
    hfall[...] = hour_rows(mhall[...], hmat[...])
    hmat[...] = gram(hfall[...]) * gcm[...]
    o_base = take(2)

    def swap_o(s):
        lanes = slice(s * half, (s + 1) * half)
        return remote(owned.at[:, lanes], owned_in.at[:, lanes], o_base + s, other_bins)

    def pause_points(s):
        lanes = slice(s * half, (s + 1) * half)

        def pause():
            wait_all(NH, send_mp(s))
            total = mp[my_b, lanes]
            for d in range(1, NH):
                total = total + mp_in[d, :, lanes]
            owned[:, lanes] = total
            swap_o(s).start()

        return pause

    invert(hmat, left, right, {9: pause_points(0), 13: pause_points(1)}, 2)
    swap_o(0).wait()
    swap_o(1).wait()
    pf_ref[...] = jnp.dot(
        owned[...] + owned_in[...],
        hmat[...],
        precision=HIGHEST,
        preferred_element_type=f32,
    )


def local(sizes, tensor, b_factor, c_factor):
    NP, NH, NB = sizes
    Z, Q = NP // 2, NH * NB
    tensor = jnp.swapaxes(tensor, 1, 2)
    hours, bins, points = tensor.shape
    width = c_factor.shape[1]
    brow = b_factor.shape[0]
    prow = width // (2 * Q)
    hh = hours // 2
    sems = 2 * Z + Q + 4 * NH + 8 + 6
    vm = lambda *shape: pltpu.VMEM(shape, f32)
    any_spec = pl.BlockSpec(memory_space=pltpu.HBM)
    vmem_spec = pl.BlockSpec(memory_space=pltpu.VMEM)
    out_shape = (
        jax.ShapeDtypeStruct((hours, width), f32),
        jax.ShapeDtypeStruct((brow, width), f32),
    )
    return pl.pallas_call(
        functools.partial(kernel, sizes),
        out_shape=out_shape,
        in_specs=[any_spec] * 3,
        out_specs=(vmem_spec, vmem_spec),
        scratch_shapes=[
            vm(hours, bins, points),
            vm(hours, width, points),
            vm(bins, width),
            pltpu.VMEM((2 * width, bins), bf16),
            vm(points, width),
            vm(width, points),
            vm(width, width),
            vm(prow, width),
            vm(Z, prow, width),
            vm(width, width),
            vm(width // 2, width),
            vm(width, width),
            vm(width, width),
            vm(width, 128),
            vm(hours, width),
            vm(4, hh, width // 2),
            vm(Z, hh, width // 2),
            vm(hours * NH, width),
            vm(width, hours),
            vm(hours * NH, width),
            vm(width, points),
            vm(points, width),
            vm(NH, brow, width),
            vm(brow, width),
            vm(brow, width),
            pltpu.VMEM((6 * STEP, width), bf16),
            pltpu.VMEM((6 * STEP, width), bf16),
            pltpu.SemaphoreType.DMA((hours + 2,)),
            pltpu.SemaphoreType.DMA((sems,)),
            pltpu.SemaphoreType.DMA((sems,)),
        ],
        compiler_params=pltpu.CompilerParams(
            collective_id=0,
            has_side_effects=True,
            vmem_limit_bytes=55160 * 1024,
        ),
    )(tensor, b_factor, c_factor)


def solution(mesh):
    sizes = (mesh.shape["pts"], mesh.shape["hrs"], mesh.shape["bins"])
    placed = (P("hrs", "pts", "bins"), P(("pts", "hrs"), None), P("bins", None))
    return jax.shard_map(
        functools.partial(local, sizes),
        mesh=mesh,
        in_specs=placed,
        out_specs=(P("hrs", None), P(("pts", "hrs"), None)),
        check_vma=False,
    )
```
